32 devices in a mesh: chain: 2 (over y), gx: 16 (over z, x, core).
Axes of the slice: x: 2, y: 2, z: 4, core: 2. Of those that a mesh axis runs over, the one named last changes fastest.
Arguments:
- courant: float32 [32, 128, 4, 128], P(('chain', 'gx')), parts along dimension 0, may hold values from 0.05 to 0.18
- ckpt_prev: float32 [32, 128, 4, 128], P(('chain', 'gx')), parts along dimension 0, may hold values from -6 to 6
- ckpt_cur: float32 [32, 128, 4, 128], P(('chain', 'gx')), parts along dimension 0, may hold values from -6 to 6
- adj_next: float32 [32, 128, 4, 128], P(('chain', 'gx')), parts along dimension 0, may hold values from -6 to 6
- adj_cur: float32 [32, 128, 4, 128], P(('chain', 'gx')), parts along dimension 0, may hold values from -6 to 6
- rec_x: int32 [4096], P(('chain', 'gx')), parts along dimension 0, may hold values from 0 to 255
- rec_plane: int32 [4096], P(('chain', 'gx')), parts along dimension 0, may hold values from 0 to 4095
- traces: float32 [4, 4096], P(None, ('chain', 'gx')), parts along dimension 1, may hold values from -6 to 6
- mass_kernel: float32 [256, 1024], P(None, 'gx'), may hold values from 0.003 to 0.03
Outputs:
- mass_gradient: float32 [32, 128, 4, 128], P(('chain', 'gx')), parts along dimension 0
- adjoint_first: float32 [32, 128, 4, 128], P(('chain', 'gx')), parts along dimension 0
- adjoint_second: float32 [32, 128, 4, 128], P(('chain', 'gx')), parts along dimension 0
The draws below stay inside these ranges and needn't reach their ends.
There are 2 independent parts, one for each index of `chain`. The reference program is written for one: setup_inputs(seed, part) draws one part's arguments, and reference() takes and returns one part's arrays. A program takes and returns all parts, laid end to end along the dimension named above; an argument that names none is the same for every part. Nothing has to cross between parts.
Inputs may be any that keep to these rules, and one draw needn't show every extreme that they name: `rec_x`: several receivers may share a cell; some x ranges hold many more receivers than others.
All inputs are finite; a program needn't handle non-finite values.
Results may differ from the reference program's by a relative error of at most 0.00007.
Values sent between devices are 32-bit elements; how exact they have to be, the bound alone decides.
A program may use at most 64 MiB of HBM per device.

```python
import math
import jax
import jax.numpy as jnp
import numpy as np

TX = 128
TY = 128
GY = 8
NZ = 4
STEPS = 4
TILES = 16
NXB = 2
NX = 256
NY = 1024
NREC = 2048


def with_ends(entries, stream_key, smallest, largest):
    place = [jax.random.randint(jax.random.fold_in(stream_key, axis), (), 0, length) for axis, length in enumerate(entries.shape)]
    main_axis = entries.shape.index(max(entries.shape))
    neighbour = place[:main_axis] + [(place[main_axis] + 1) % entries.shape[main_axis]] + place[main_axis + 1:]
    return entries.at[tuple(place)].set(smallest).at[tuple(neighbour)].set(largest)


def shard_levels(rng, extent, cuts, least, top_value):
    def one(position, shards_of):
        steps = jax.random.uniform(jax.random.fold_in(jax.random.fold_in(rng, 6), position), (shards_of,), jnp.float32, least / len(cuts), top_value / len(cuts))
        return jnp.repeat(jnp.exp(steps), extent[position] // shards_of).reshape((-1,) + (1,) * (len(extent) - position - 1))

    loudness = one(*cuts[0])
    for cut in cuts[1:]:
        loudness = loudness * one(*cut)
    return loudness


def rank_table(amount, slope):
    loads = [(1 << 20) // math.isqrt(grade ** slope) + 1 for grade in range(1, amount + 1)]
    deviation = 1 + sum(loads) // (1 << 30)
    return np.cumsum(np.array([max(1, weight // deviation) for weight in loads]))


def ranked(own_key, extent, count, skew):
    listing = rank_table(count, skew)
    lot = jax.random.randint(jax.random.fold_in(own_key, 1), extent, 0, int(listing[count - 1]))
    rank = jnp.searchsorted(jnp.asarray(listing, jnp.int32), lot, side="right")
    return jax.random.permutation(jax.random.fold_in(own_key, 2), count)[rank].astype(jnp.int32)


def scatter_about(key, shape, scale, most, cuts=(), kind=jnp.bfloat16):
    array = scale * jax.random.normal(key, shape, jnp.float32)
    if cuts:
        array = array * shard_levels(key, shape, cuts, -0.22, 0.18)
    return jnp.clip(array, -most, most).astype(kind)


def setup_inputs(seed: int = 0, part: int = 0) -> dict:
    seeds = jax.random.split(jax.random.key(seed), 10)
    part_splits = jax.random.split(jax.random.fold_in(seeds[9], part), 10)
    return {
        "courant": jnp.clip(0.05 + 0.13000001 * jax.random.uniform(part_splits[0], (TILES, TX, NZ, TY), jnp.float32) ** shard_levels(part_splits[0], (TILES, TX, NZ, TY), ((0, 16),), -0.2, 0.2), 0.05, 0.18),
        "ckpt_prev": scatter_about(part_splits[1], (TILES, TX, NZ, TY), 1.0, 6.0, ((0, 16),), jnp.float32),
        "ckpt_cur": scatter_about(part_splits[2], (TILES, TX, NZ, TY), 1.0, 6.0, ((0, 16),), jnp.float32),
        "adj_next": scatter_about(part_splits[3], (TILES, TX, NZ, TY), 1.0, 6.0, ((0, 16),), jnp.float32),
        "adj_cur": scatter_about(part_splits[4], (TILES, TX, NZ, TY), 1.0, 6.0, ((0, 16),), jnp.float32),
        "rec_x": with_ends(ranked(part_splits[5], (NREC,), NX, 2), jax.random.fold_in(part_splits[5], 3), 0, NX - 1).astype(jnp.int32),
        "rec_plane": with_ends(jax.random.randint(part_splits[6], (NREC,), 0, NZ * NY), jax.random.fold_in(part_splits[6], 1), 0, (NZ * NY) - 1).astype(jnp.int32),
        "traces": scatter_about(part_splits[7], (STEPS, NREC), 1.0, 6.0, ((1, 16),), jnp.float32),
        "mass_kernel": jnp.clip(jnp.exp(math.log(0.03) - 2.3025851 * jax.random.uniform(seeds[8], (NX, NY), jnp.float32) ** shard_levels(seeds[8], (NX, NY), ((1, 16),), -0.2, 0.2)), 0.003, 0.03),
    }


STENCIL_COEF = (-205.0 / 72.0, 8.0 / 5.0, -1.0 / 5.0, 8.0 / 315.0, -1.0 / 560.0)


def laplace_core(extended):
    padded = jnp.pad(extended, ((0, 0), (4, 4), (0, 0)))
    x_rows = extended.shape[0] - 8
    z_depth = extended.shape[1]
    y_cols = extended.shape[2] - 8

    def shifted(move_x, move_z, move_y):
        return padded[4 + move_x:4 + move_x + x_rows, 4 + move_z:4 + move_z + z_depth, 4 + move_y:4 + move_y + y_cols]

    result = (3.0 * STENCIL_COEF[0]) * shifted(0, 0, 0)
    for offset in range(1, 5):
        pair_sum = shifted(offset, 0, 0) + shifted(-offset, 0, 0)
        pair_sum = pair_sum + shifted(0, offset, 0) + shifted(0, -offset, 0)
        pair_sum = pair_sum + shifted(0, 0, offset) + shifted(0, 0, -offset)
        result = result + STENCIL_COEF[offset] * pair_sum
    return result


def full_laplace(field):
    return laplace_core(jnp.pad(field, ((4, 4), (0, 0), (4, 4))))


def to_grid(tiled):
    return tiled.reshape(NXB, GY, TX, NZ, TY).transpose(0, 2, 3, 1, 4).reshape(NX, NZ, NY)


def to_tiles(grid):
    return grid.reshape(NXB, TX, NZ, GY, TY).transpose(0, 3, 1, 2, 4).reshape(TILES, TX, NZ, TY)


def reference(courant, ckpt_prev, ckpt_cur, adj_next, adj_cur, rec_x, rec_plane, traces, mass_kernel):
    model = to_grid(courant)
    u_prev, u_cur = to_grid(ckpt_prev), to_grid(ckpt_cur)
    images = []
    for section in range(STEPS):
        laplacian = full_laplace(u_cur)
        images.append(laplacian)
        if section + 1 < STEPS:
            u_prev, u_cur = u_cur, 2.0 * u_cur - u_prev + model * laplacian
    cell_index = rec_x.astype(jnp.int32) * (NZ * NY) + rec_plane.astype(jnp.int32)
    adj_later, adj_now = to_grid(adj_next), to_grid(adj_cur)
    gradient = jnp.zeros_like(model)
    for section in reversed(range(STEPS)):
        gradient = gradient + adj_now * images[section]
        earlier = 2.0 * adj_now - adj_later + full_laplace(model * adj_now)
        earlier = earlier.reshape(-1).at[cell_index].add(traces[section]).reshape(adj_now.shape)
        adj_later, adj_now = adj_now, earlier
    spectrum = jnp.fft.fft2(gradient, axes=(0, 2))
    scaled = jnp.fft.ifft2(spectrum * mass_kernel[:, None, :], axes=(0, 2))
    mass_gradient = jnp.real(scaled).astype(jnp.float32)
    return to_tiles(mass_gradient), to_tiles(adj_now), to_tiles(adj_later)
```

```python
import functools
import math

import jax
import jax.numpy as jnp
import numpy as np
from jax import lax
from jax.experimental import pallas as pl
from jax.experimental.pallas import tpu as pltpu
from jax.sharding import PartitionSpec as P

GY = 8
STEPS = 4


STENCIL_COEF = (-205.0 / 72.0, 8.0 / 5.0, -1.0 / 5.0, 8.0 / 315.0, -1.0 / 560.0)


MESH = pl.DeviceIdType.MESH
HIGHEST = lax.Precision.HIGHEST


def dot_f32(left, right, left_dim=1, right_dim=0):
    return lax.dot_general(
        left,
        right,
        (((left_dim,), (right_dim,)), ((), ())),
        precision=HIGHEST,
        preferred_element_type=jnp.float32,
    )


def stencil_tables(z_depth, y_cols, chunk):
    coef = np.array(STENCIL_COEF, np.float64)
    halo = 4 * z_depth
    row = np.arange(chunk)[:, None]
    col = np.arange(chunk + 2 * halo)[None, :] - halo
    dx = np.abs(row // z_depth - col // z_depth)
    dz = np.abs(row % z_depth - col % z_depth)
    band = np.where((dz == 0) & (dx <= 4), coef[np.minimum(dx, 4)], 0.0)
    band = band + np.where((dx == 0) & (dz <= 4), coef[np.minimum(dz, 4)], 0.0)
    lane = np.arange(y_cols)
    dy = np.abs(lane[:, None] - lane[None, :])
    along_y = np.where(dy <= 4, coef[np.minimum(dy, 4)], 0.0)
    along_y = np.kron(np.eye(2), along_y)
    edge = np.arange(halo)
    near = edge[:, None] // z_depth + 4 - edge[None, :] // z_depth
    same = edge[:, None] % z_depth == edge[None, :] % z_depth
    from_low = np.where(same & (near <= 4), coef[np.minimum(near, 4)], 0.0)
    far = 4 + edge[None, :] // z_depth - edge[:, None] // z_depth
    from_high = np.where(same & (far <= 4), coef[np.minimum(far, 4)], 0.0)
    rim = np.zeros((16, 2 * y_cols))
    for field in range(2):
        for depth in range(4):
            for y in range(4):
                if y + 4 - depth <= 4:
                    rim[field * 4 + depth, field * y_cols + y] = coef[y + 4 - depth]
                last = y_cols - 1 - y
                gap = y_cols + depth - last
                if gap <= 4:
                    rim[8 + field * 4 + depth, field * y_cols + last] = coef[gap]
    pick = np.zeros((16, 2 * y_cols))
    for field in range(2):
        for depth in range(4):
            pick[field * 4 + depth, field * y_cols + depth] = 1.0
            pick[8 + field * 4 + depth, field * y_cols + y_cols - 4 + depth] = 1.0
    tables = (band, along_y, from_low, from_high, rim, pick)
    return [jnp.asarray(table.astype(np.float32)) for table in tables]


def window_kernel(
    chunk,
    model_ref, prev_ref, cur_ref, next_ref, now_ref, rec_ref,
    band_ref, along_ref, low_ref, high_ref, rim_ref, pick_ref,
    grad_ref, first_ref, second_ref,
    both, lap, images, waves, adjoints, records, hot, weights, inject,
    x_out, x_in, y_out, y_in, halo_send, halo_recv, rec_send, rec_recv, own_sem,
):
    chain = lax.axis_index("chain")
    tile = lax.axis_index("gx")
    devices = lax.axis_size("gx")
    x_blocks = devices // GY
    rows, y_cols = model_ref.shape
    halo = x_out.shape[2]
    column = lax.rem(tile, GY)
    block = tile // GY
    neighbours = (
        lax.rem(block + x_blocks - 1, x_blocks) * GY + column,
        lax.rem(block + 1, x_blocks) * GY + column,
        block * GY + lax.rem(column + GY - 1, GY),
        block * GY + lax.rem(column + 1, GY),
    )
    has_low = (block > 0).astype(jnp.float32)
    has_high = (block < x_blocks - 1).astype(jnp.float32)
    has_left = (column > 0).astype(jnp.float32)
    has_right = (column < GY - 1).astype(jnp.float32)

    own = pltpu.make_async_copy(rec_ref, records.at[0], own_sem)
    own.start()
    barrier = pltpu.get_barrier_semaphore()

    @pl.loop(1, devices)
    def _(step):
        pl.semaphore_signal(
            barrier, inc=1, device_id=(chain, lax.rem(tile + step, devices)), device_id_type=MESH
        )

    both[0:halo, :] = jnp.zeros((halo, 2 * y_cols), jnp.float32)
    both[halo + rows :, :] = jnp.zeros((halo, 2 * y_cols), jnp.float32)
    low_rows = lax.broadcasted_iota(jnp.int32, rim_ref.shape, 0) < 8
    rim = rim_ref[...] * jnp.where(low_rows, has_left, has_right)

    def pack(phase, wave, adjoint):
        both[halo : halo + rows, 0:y_cols] = wave
        both[halo : halo + rows, y_cols:] = model_ref[...] * adjoint
        x_out[phase, 0] = both[halo : 2 * halo, :]
        x_out[phase, 1] = both[rows : halo + rows, :]
        strips = dot_f32(pick_ref[...], both[halo : halo + rows, :], 1, 1)
        y_out[phase, 0] = strips[0:8]
        y_out[phase, 1] = strips[8:16]

    def halo_copies(phase):
        copies = []
        for way in range(4):
            source = x_out if way < 2 else y_out
            target = x_in if way < 2 else y_in
            copies.append(
                pltpu.make_async_remote_copy(
                    src_ref=source.at[phase, way % 2],
                    dst_ref=target.at[phase, 1 - way % 2],
                    send_sem=halo_send.at[phase, way],
                    recv_sem=halo_recv.at[phase, way],
                    device_id=(chain, neighbours[way]),
                    device_id_type=MESH,
                )
            )
        return copies

    def record_copy(step):
        return pltpu.make_async_remote_copy(
            src_ref=rec_ref,
            dst_ref=records.at[step],
            send_sem=rec_send.at[step],
            recv_sem=rec_recv.at[step],
            device_id=(chain, lax.rem(tile + step, devices)),
            device_id_type=MESH,
        )

    pack(0, cur_ref[...], now_ref[...])
    pl.semaphore_wait(barrier, devices - 1)
    pending = []
    width = rec_ref.shape[1]
    total = devices * width
    part = math.gcd(total, 2048)
    for phase in range(STEPS):
        copies = halo_copies(phase)
        for copy in copies:
            copy.start()
        pending += copies
        if phase == 0:

            @pl.loop(1, devices)
            def _(step):
                record_copy(step).start()

        lap[...] = dot_f32(both[halo : halo + rows, :], along_ref[...])
        for start in range(0, rows, chunk):
            lap[start : start + chunk, :] += dot_f32(
                band_ref[...], both[start : start + chunk + 2 * halo, :]
            )
        if phase == 0:
            own.wait()

            @pl.loop(1, devices)
            def _(step):
                record_copy(step).wait()

            @pl.loop(0, devices)
            def _(step):
                lanes = pl.ds(pl.multiple_of(step * width, width), width)
                cell = records[step, 0:1, :] - (tile * rows).astype(jnp.float32)
                index = lax.broadcasted_iota(jnp.int32, (rows, width), 0).astype(jnp.float32)
                hot[:, lanes] = jnp.where(index == cell, 1.0, 0.0).astype(jnp.bfloat16)

        section = STEPS - 1 - phase

        @pl.loop(0, devices)
        def _(step):
            lanes = pl.ds(pl.multiple_of(step * width, width), width)
            place = records[step, 1:2, :]
            value = records[step, 2 + section : 3 + section, :]
            index = lax.broadcasted_iota(jnp.int32, (y_cols, width), 0).astype(jnp.float32)
            rest = jnp.where(index == place, value, 0.0)
            for level in range(3):
                piece = rest.astype(jnp.bfloat16)
                weights[level * y_cols : (level + 1) * y_cols, lanes] = piece
                rest = rest - piece.astype(jnp.float32)

        def injected(lanes):
            triple = lax.dot_general(
                hot[:, lanes],
                weights[:, lanes],
                (((1,), (1,)), ((), ())),
                preferred_element_type=jnp.float32,
            )
            return (
                triple[:, 0:y_cols]
                + triple[:, y_cols : 2 * y_cols]
                + triple[:, 2 * y_cols :]
            )

        inject[...] = injected(pl.ds(0, part))
        if total > part:

            @pl.loop(1, total // part)
            def _(step):
                inject[...] += injected(pl.ds(pl.multiple_of(step * part, part), part))

        for copy in copies:
            copy.wait_recv()
        sides = jnp.concatenate((y_in[phase, 0], y_in[phase, 1]), axis=0)
        lap[...] += dot_f32(sides, rim, 0, 0)
        lap[0:halo, :] += has_low * dot_f32(low_ref[...], x_in[phase, 0])
        lap[rows - halo :, :] += has_high * dot_f32(high_ref[...], x_in[phase, 1])
        image = lap[:, 0:y_cols]
        images[phase] = image
        if phase + 1 < STEPS:
            older = prev_ref[...] if phase == 0 else (cur_ref[...] if phase == 1 else waves[0])
            newer = cur_ref[...] if phase == 0 else waves[phase - 1]
            waves[phase] = 2.0 * newer - older + model_ref[...] * image
        later = next_ref[...] if phase == 0 else (now_ref[...] if phase == 1 else adjoints[phase - 2])
        now = now_ref[...] if phase == 0 else adjoints[phase - 1]
        adjoints[phase] = 2.0 * now - later + lap[:, y_cols:] + inject[...]
        if phase + 1 < STEPS:
            pack(phase + 1, waves[phase], adjoints[phase])
    grad_ref[...] = (
        now_ref[...] * images[3]
        + adjoints[0] * images[2]
        + adjoints[1] * images[1]
        + adjoints[2] * images[0]
    )
    first_ref[...] = adjoints[3]
    second_ref[...] = adjoints[2]
    for copy in pending:
        copy.wait_send()


def run_window(model, u_prev, u_cur, a_next, a_cur, records):
    rows, y_cols = model.shape
    z_depth = 4
    devices = lax.axis_size("gx")
    halo = 4 * z_depth
    chunk = 128
    total = devices * records.shape[1]
    tables = stencil_tables(z_depth, y_cols, chunk)
    field = jax.ShapeDtypeStruct((rows, y_cols), jnp.float32)
    vmem = pl.BlockSpec(memory_space=pltpu.VMEM)
    return pl.pallas_call(
        functools.partial(window_kernel, chunk),
        out_shape=(field, field, field),
        in_specs=[vmem] * 12,
        out_specs=(vmem, vmem, vmem),
        scratch_shapes=[
            pltpu.VMEM((rows + 2 * halo, 2 * y_cols), jnp.float32),
            pltpu.VMEM((rows, 2 * y_cols), jnp.float32),
            pltpu.VMEM((STEPS, rows, y_cols), jnp.float32),
            pltpu.VMEM((STEPS - 1, rows, y_cols), jnp.float32),
            pltpu.VMEM((STEPS, rows, y_cols), jnp.float32),
            pltpu.VMEM((devices,) + records.shape, jnp.float32),
            pltpu.VMEM((rows, total), jnp.bfloat16),
            pltpu.VMEM((3 * y_cols, total), jnp.bfloat16),
            pltpu.VMEM((rows, y_cols), jnp.float32),
            pltpu.VMEM((STEPS, 2, halo, 2 * y_cols), jnp.float32),
            pltpu.VMEM((STEPS, 2, halo, 2 * y_cols), jnp.float32),
            pltpu.VMEM((STEPS, 2, 8, rows), jnp.float32),
            pltpu.VMEM((STEPS, 2, 8, rows), jnp.float32),
            pltpu.SemaphoreType.DMA((STEPS, 4)),
            pltpu.SemaphoreType.DMA((STEPS, 4)),
            pltpu.SemaphoreType.DMA((devices,)),
            pltpu.SemaphoreType.DMA((devices,)),
            pltpu.SemaphoreType.DMA,
        ],
        compiler_params=pltpu.CompilerParams(
            collective_id=0, has_side_effects=True, vmem_limit_bytes=56 * 2**20
        ),
    )(model, u_prev, u_cur, a_next, a_cur, records, *tables)


def pick_factor(length):
    candidate = math.isqrt(length)
    if candidate * candidate < length:
        candidate = candidate + 1
    while length % candidate != 0:
        candidate = candidate + 1
    return candidate


def phase_tables(rows_count, cols_count, modulus):
    first = jnp.arange(rows_count, dtype=jnp.int32)
    second = jnp.arange(cols_count, dtype=jnp.int32)
    phase_int = first[:, None] * second[None, :] % modulus
    angle_rad = phase_int.astype(jnp.float32) * (2.0 * math.pi / modulus)
    return (jnp.cos(angle_rad), jnp.sin(angle_rad))


def complex_mix(form, tab_cos, tab_sin, real_part, imag_part, orient):

    def product(table, data):
        return jnp.einsum(
            form, table, data, precision=lax.Precision.HIGHEST, preferred_element_type=jnp.float32
        )

    out_real = product(tab_cos, real_part) - orient * product(tab_sin, imag_part)
    out_imag = product(tab_cos, imag_part) + orient * product(tab_sin, real_part)
    return (out_real, out_imag)


def transform_rows(real_part, imag_part, orient):
    length, width = real_part.shape
    outer_len = pick_factor(length)
    inner_len = length // outer_len
    data_re = real_part.reshape(outer_len, inner_len, width)
    data_im = imag_part.reshape(outer_len, inner_len, width)
    cos_outer, sin_outer = phase_tables(outer_len, outer_len, outer_len)
    mid_re, mid_im = complex_mix("ca,abm->cbm", cos_outer, sin_outer, data_re, data_im, orient)
    twist_cos, twist_sin = phase_tables(outer_len, inner_len, length)
    twist_cos = twist_cos[:, :, None]
    twist_sin = twist_sin[:, :, None]
    turned_re = mid_re * twist_cos - orient * mid_im * twist_sin
    turned_im = mid_im * twist_cos + orient * mid_re * twist_sin
    cos_inner, sin_inner = phase_tables(inner_len, inner_len, inner_len)
    final_re, final_im = complex_mix(
        "db,cbm->dcm", cos_inner, sin_inner, turned_re, turned_im, orient
    )
    return (final_re.reshape(length, width), final_im.reshape(length, width))


def per_device(
    courant, ckpt_prev, ckpt_cur, adj_next, adj_cur, rec_x, rec_plane, traces, mass_kernel
):
    x_rows, z_depth, y_cols = courant.shape[1:]
    devices = lax.axis_size("gx")
    x_blocks = devices // GY
    x_total = x_rows * x_blocks
    y_total = y_cols * GY
    cell_y = rec_plane % y_total
    cell_z = rec_plane // y_total
    owner = rec_x // x_rows * GY + cell_y // y_cols
    cell_row = (owner * x_rows + rec_x % x_rows) * z_depth + cell_z
    records = jnp.concatenate(
        (
            cell_row.astype(jnp.float32)[None],
            (cell_y % y_cols).astype(jnp.float32)[None],
            traces,
            jnp.zeros((6 - STEPS, rec_x.shape[0]), jnp.float32),
        ),
        axis=0,
    )
    gradient, adj_now, adj_later = run_window(
        *(
            field.reshape(x_rows * z_depth, y_cols)
            for field in (courant, ckpt_prev, ckpt_cur, adj_next, adj_cur)
        ),
        records,
    )
    tile_shape = (1, x_rows, z_depth, y_cols)
    flat_grad = gradient.reshape(x_rows * z_depth, 1, y_cols)
    rows = lax.all_to_all(flat_grad, "gx", split_axis=0, concat_axis=1, tiled=True)
    share = rows.shape[0]
    lines = rows.reshape(share * x_blocks, y_total).T
    spec_re_t, spec_im_t = transform_rows(lines, jnp.zeros_like(lines), -1.0)
    spec_re = spec_re_t.T.reshape(share, x_blocks, y_total)
    spec_im = spec_im_t.T.reshape(share, x_blocks, y_total)
    cols_re, cols_im = (
        lax.all_to_all(spec_re, "gx", split_axis=2, concat_axis=0, tiled=True),
        lax.all_to_all(spec_im, "gx", split_axis=2, concat_axis=0, tiled=True),
    )
    col_width = cols_re.shape[2]
    half_width = z_depth * col_width

    def to_columns(part):
        return (
            part.reshape(x_rows, z_depth, x_blocks, col_width)
            .transpose(2, 0, 1, 3)
            .reshape(x_total, half_width)
        )

    def from_columns(part):
        return (
            part.reshape(x_blocks, x_rows, z_depth, col_width)
            .transpose(1, 2, 0, 3)
            .reshape(devices * share, x_blocks, col_width)
        )

    freq_re, freq_im = transform_rows(to_columns(cols_re), to_columns(cols_im), -1.0)
    kernel_scale = (
        jnp.broadcast_to(mass_kernel[:, None, :], (x_total, z_depth, col_width)).reshape(
            x_total, half_width
        )
        / x_total
    )
    freq_re = freq_re * kernel_scale
    freq_im = freq_im * kernel_scale
    spat_re, spat_im = transform_rows(freq_re, freq_im, 1.0)
    back_re = from_columns(spat_re)
    back_im = from_columns(spat_im)
    line_re, line_im = (
        lax.all_to_all(back_re, "gx", split_axis=0, concat_axis=2, tiled=True),
        lax.all_to_all(back_im, "gx", split_axis=0, concat_axis=2, tiled=True),
    )
    lines_re = line_re.reshape(share * x_blocks, y_total).T
    lines_im = line_im.reshape(share * x_blocks, y_total).T
    real_t, imag_t = transform_rows(lines_re, lines_im, 1.0)
    real_lines = (real_t.T / y_total).reshape(share, devices, y_cols)
    tiled = lax.all_to_all(real_lines, "gx", split_axis=1, concat_axis=0, tiled=True)
    return (tiled.reshape(tile_shape), adj_now.reshape(tile_shape), adj_later.reshape(tile_shape))


def solution(mesh):
    in_specs = (
        P(("chain", "gx"), None, None, None),
        P(("chain", "gx"), None, None, None),
        P(("chain", "gx"), None, None, None),
        P(("chain", "gx"), None, None, None),
        P(("chain", "gx"), None, None, None),
        P(("chain", "gx")),
        P(("chain", "gx")),
        P(None, ("chain", "gx")),
        P(None, "gx"),
    )
    out_specs = (
        P(("chain", "gx"), None, None, None),
        P(("chain", "gx"), None, None, None),
        P(("chain", "gx"), None, None, None),
    )
    return jax.shard_map(
        per_device, mesh=mesh, in_specs=in_specs, out_specs=out_specs, check_vma=False
    )
```

```python
import functools
import math

import jax
import jax.numpy as jnp
import numpy as np
from jax import lax
from jax.experimental import pallas as pl
from jax.experimental.pallas import tpu as pltpu
from jax.sharding import PartitionSpec as P

GY = 8
STEPS = 4


STENCIL_COEF = (-205.0 / 72.0, 8.0 / 5.0, -1.0 / 5.0, 8.0 / 315.0, -1.0 / 560.0)


MESH = pl.DeviceIdType.MESH
HIGHEST = lax.Precision.HIGHEST


def dot_f32(left, right, left_dim=1, right_dim=0):
    return lax.dot_general(
        left,
        right,
        (((left_dim,), (right_dim,)), ((), ())),
        precision=HIGHEST,
        preferred_element_type=jnp.float32,
    )


def stencil_tables(z_depth, y_cols, chunk):
    coef = np.array(STENCIL_COEF, np.float64)
    halo = 4 * z_depth
    row = np.arange(chunk)[:, None]
    col = np.arange(chunk + 2 * halo)[None, :] - halo
    dx = np.abs(row // z_depth - col // z_depth)
    dz = np.abs(row % z_depth - col % z_depth)
    band = np.where((dz == 0) & (dx <= 4), coef[np.minimum(dx, 4)], 0.0)
    band = band + np.where((dx == 0) & (dz <= 4), coef[np.minimum(dz, 4)], 0.0)
    lane = np.arange(y_cols)
    dy = np.abs(lane[:, None] - lane[None, :])
    along_y = np.where(dy <= 4, coef[np.minimum(dy, 4)], 0.0)
    along_y = np.kron(np.eye(2), along_y)
    edge = np.arange(halo)
    near = edge[:, None] // z_depth + 4 - edge[None, :] // z_depth
    same = edge[:, None] % z_depth == edge[None, :] % z_depth
    from_low = np.where(same & (near <= 4), coef[np.minimum(near, 4)], 0.0)
    far = 4 + edge[None, :] // z_depth - edge[:, None] // z_depth
    from_high = np.where(same & (far <= 4), coef[np.minimum(far, 4)], 0.0)
    rim = np.zeros((16, 2 * y_cols))
    for field in range(2):
        for depth in range(4):
            for y in range(4):
                if y + 4 - depth <= 4:
                    rim[field * 4 + depth, field * y_cols + y] = coef[y + 4 - depth]
                last = y_cols - 1 - y
                gap = y_cols + depth - last
                if gap <= 4:
                    rim[8 + field * 4 + depth, field * y_cols + last] = coef[gap]
    pick = np.zeros((16, 2 * y_cols))
    for field in range(2):
        for depth in range(4):
            pick[field * 4 + depth, field * y_cols + depth] = 1.0
            pick[8 + field * 4 + depth, field * y_cols + y_cols - 4 + depth] = 1.0
    tables = (band, along_y, from_low, from_high, rim, pick)
    return [jnp.asarray(table.astype(np.float32)) for table in tables]


def plane_and_part(tile, planes):
    share = GY // planes
    column = lax.rem(tile, GY)
    return column // share, tile // GY * share + lax.rem(column, share)


def plane_holder(plane, part, planes):
    share = GY // planes
    return part // share * GY + plane * share + lax.rem(part, share)


def window_kernel(
    chunk, move_mass,
    model_ref, prev_ref, cur_ref, next_ref, now_ref, rec_ref, mass_ref,
    band_ref, along_ref, low_ref, high_ref, rim_ref, pick_ref,
    grad_ref, first_ref, second_ref, mass_out,
    both, lap, images, waves, adjoints, records, hot, weights, inject,
    x_out, x_in, y_out, y_in, halo_send, halo_recv, rec_send, rec_recv, own_sem,
    mass_in, mass_send, mass_recv, mass_own,
):
    chain = lax.axis_index("chain")
    tile = lax.axis_index("gx")
    devices = lax.axis_size("gx")
    x_blocks = devices // GY
    rows, y_cols = model_ref.shape
    halo = x_out.shape[2]
    column = lax.rem(tile, GY)
    block = tile // GY
    neighbours = (
        lax.rem(block + x_blocks - 1, x_blocks) * GY + column,
        lax.rem(block + 1, x_blocks) * GY + column,
        block * GY + lax.rem(column + GY - 1, GY),
        block * GY + lax.rem(column + 1, GY),
    )
    has_low = (block > 0).astype(jnp.float32)
    has_high = (block < x_blocks - 1).astype(jnp.float32)
    has_left = (column > 0).astype(jnp.float32)
    has_right = (column < GY - 1).astype(jnp.float32)

    own = pltpu.make_async_copy(rec_ref, records.at[0], own_sem)
    own.start()
    barrier = pltpu.get_barrier_semaphore()

    @pl.loop(1, devices)
    def _(step):
        pl.semaphore_signal(
            barrier, inc=1, device_id=(chain, lax.rem(tile + step, devices)), device_id_type=MESH
        )

    both[0:halo, :] = jnp.zeros((halo, 2 * y_cols), jnp.float32)
    both[halo + rows :, :] = jnp.zeros((halo, 2 * y_cols), jnp.float32)
    low_rows = lax.broadcasted_iota(jnp.int32, rim_ref.shape, 0) < 8
    rim = rim_ref[...] * jnp.where(low_rows, has_left, has_right)

    def pack(phase, wave, adjoint):
        both[halo : halo + rows, 0:y_cols] = wave
        both[halo : halo + rows, y_cols:] = model_ref[...] * adjoint
        x_out[phase, 0] = both[halo : 2 * halo, :]
        x_out[phase, 1] = both[rows : halo + rows, :]
        strips = dot_f32(pick_ref[...], both[halo : halo + rows, :], 1, 1)
        y_out[phase, 0] = strips[0:8]
        y_out[phase, 1] = strips[8:16]

    def halo_copies(phase):
        copies = []
        for way in range(4):
            source = x_out if way < 2 else y_out
            target = x_in if way < 2 else y_in
            copies.append(
                pltpu.make_async_remote_copy(
                    src_ref=source.at[phase, way % 2],
                    dst_ref=target.at[phase, 1 - way % 2],
                    send_sem=halo_send.at[phase, way],
                    recv_sem=halo_recv.at[phase, way],
                    device_id=(chain, neighbours[way]),
                    device_id_type=MESH,
                )
            )
        return copies

    def record_copy(step):
        return pltpu.make_async_remote_copy(
            src_ref=rec_ref,
            dst_ref=records.at[step],
            send_sem=rec_send.at[step],
            recv_sem=rec_recv.at[step],
            device_id=(chain, lax.rem(tile + step, devices)),
            device_id_type=MESH,
        )

    slots = mass_in.shape[0]
    _, quarter = plane_and_part(tile, slots)

    def mass_copies(number):
        target = plane_holder(number, tile // slots, slots)
        remote = pltpu.make_async_remote_copy(
            src_ref=mass_ref,
            dst_ref=mass_in.at[lax.rem(tile, slots)],
            send_sem=mass_send.at[number],
            recv_sem=mass_recv.at[lax.rem(tile, slots)],
            device_id=(chain, target),
            device_id_type=MESH,
        )
        local = pltpu.make_async_copy(mass_ref, mass_in.at[lax.rem(tile, slots)], mass_own)
        return target != tile, remote, local

    def mass_start():
        for number in range(slots):
            away, remote, local = mass_copies(number)
            pl.when(away)(remote.start)
            pl.when(jnp.logical_not(away))(local.start)

    def mass_finish():
        for number in range(slots):
            away, remote, local = mass_copies(number)
            pl.when(away)(remote.wait_send)
            pl.when(jnp.logical_not(away))(local.wait)
        for slot in range(slots):
            arrival = pltpu.make_async_remote_copy(
                src_ref=mass_ref,
                dst_ref=mass_in.at[slot],
                send_sem=mass_send.at[slot],
                recv_sem=mass_recv.at[slot],
                device_id=(chain, lax.rem(tile + 1, devices)),
                device_id_type=MESH,
            )
            pl.when(quarter * slots + slot != tile)(arrival.wait_recv)
        mass_out[...] = mass_in[...]

    pack(0, cur_ref[...], now_ref[...])
    pl.semaphore_wait(barrier, devices - 1)
    pending = []
    width = rec_ref.shape[1]
    total = devices * width
    part = math.gcd(total, 2048)
    for phase in range(STEPS):
        copies = halo_copies(phase)
        for copy in copies:
            copy.start()
        pending += copies
        if phase == 0:

            @pl.loop(1, devices)
            def _(step):
                record_copy(step).start()

            if move_mass:
                mass_start()

        lap[...] = dot_f32(both[halo : halo + rows, :], along_ref[...])
        for start in range(0, rows, chunk):
            lap[start : start + chunk, :] += dot_f32(
                band_ref[...], both[start : start + chunk + 2 * halo, :]
            )
        if phase == 0:
            own.wait()

            @pl.loop(1, devices)
            def _(step):
                record_copy(step).wait()

            @pl.loop(0, devices)
            def _(step):
                lanes = pl.ds(pl.multiple_of(step * width, width), width)
                cell = records[step, 0:1, :] - (tile * rows).astype(jnp.float32)
                index = lax.broadcasted_iota(jnp.int32, (rows, width), 0).astype(jnp.float32)
                hot[:, lanes] = jnp.where(index == cell, 1.0, 0.0).astype(jnp.bfloat16)

        section = STEPS - 1 - phase

        @pl.loop(0, devices)
        def _(step):
            lanes = pl.ds(pl.multiple_of(step * width, width), width)
            place = records[step, 1:2, :]
            value = records[step, 2 + section : 3 + section, :]
            index = lax.broadcasted_iota(jnp.int32, (y_cols, width), 0).astype(jnp.float32)
            rest = jnp.where(index == place, value, 0.0)
            for level in range(3):
                piece = rest.astype(jnp.bfloat16)
                weights[level * y_cols : (level + 1) * y_cols, lanes] = piece
                rest = rest - piece.astype(jnp.float32)

        def injected(lanes):
            triple = lax.dot_general(
                hot[:, lanes],
                weights[:, lanes],
                (((1,), (1,)), ((), ())),
                preferred_element_type=jnp.float32,
            )
            return (
                triple[:, 0:y_cols]
                + triple[:, y_cols : 2 * y_cols]
                + triple[:, 2 * y_cols :]
            )

        inject[...] = injected(pl.ds(0, part))
        if total > part:

            @pl.loop(1, total // part)
            def _(step):
                inject[...] += injected(pl.ds(pl.multiple_of(step * part, part), part))

        for copy in copies:
            copy.wait_recv()
        sides = jnp.concatenate((y_in[phase, 0], y_in[phase, 1]), axis=0)
        lap[...] += dot_f32(sides, rim, 0, 0)
        lap[0:halo, :] += has_low * dot_f32(low_ref[...], x_in[phase, 0])
        lap[rows - halo :, :] += has_high * dot_f32(high_ref[...], x_in[phase, 1])
        image = lap[:, 0:y_cols]
        images[phase] = image
        if phase + 1 < STEPS:
            older = prev_ref[...] if phase == 0 else (cur_ref[...] if phase == 1 else waves[0])
            newer = cur_ref[...] if phase == 0 else waves[phase - 1]
            waves[phase] = 2.0 * newer - older + model_ref[...] * image
        later = next_ref[...] if phase == 0 else (now_ref[...] if phase == 1 else adjoints[phase - 2])
        now = now_ref[...] if phase == 0 else adjoints[phase - 1]
        adjoints[phase] = 2.0 * now - later + lap[:, y_cols:] + inject[...]
        if phase + 1 < STEPS:
            pack(phase + 1, waves[phase], adjoints[phase])
    grad_ref[...] = (
        now_ref[...] * images[3]
        + adjoints[0] * images[2]
        + adjoints[1] * images[1]
        + adjoints[2] * images[0]
    )
    first_ref[...] = adjoints[3]
    second_ref[...] = adjoints[2]
    for copy in pending:
        copy.wait_send()
    if move_mass:
        mass_finish()
    else:
        mass_out[...] = jnp.zeros(mass_out.shape, jnp.float32)


def run_window(model, u_prev, u_cur, a_next, a_cur, records, mass, move_mass):
    rows, y_cols = model.shape
    z_depth = 4
    devices = lax.axis_size("gx")
    halo = 4 * z_depth
    chunk = 128
    total = devices * records.shape[1]
    tables = stencil_tables(z_depth, y_cols, chunk)
    field = jax.ShapeDtypeStruct((rows, y_cols), jnp.float32)
    slots = jax.ShapeDtypeStruct((z_depth,) + mass.shape, jnp.float32)
    vmem = pl.BlockSpec(memory_space=pltpu.VMEM)
    return pl.pallas_call(
        functools.partial(window_kernel, chunk, move_mass),
        out_shape=(field, field, field, slots),
        in_specs=[vmem] * 13,
        out_specs=(vmem,) * 4,
        scratch_shapes=[
            pltpu.VMEM((rows + 2 * halo, 2 * y_cols), jnp.float32),
            pltpu.VMEM((rows, 2 * y_cols), jnp.float32),
            pltpu.VMEM((STEPS, rows, y_cols), jnp.float32),
            pltpu.VMEM((STEPS - 1, rows, y_cols), jnp.float32),
            pltpu.VMEM((STEPS, rows, y_cols), jnp.float32),
            pltpu.VMEM((devices,) + records.shape, jnp.float32),
            pltpu.VMEM((rows, total), jnp.bfloat16),
            pltpu.VMEM((3 * y_cols, total), jnp.bfloat16),
            pltpu.VMEM((rows, y_cols), jnp.float32),
            pltpu.VMEM((STEPS, 2, halo, 2 * y_cols), jnp.float32),
            pltpu.VMEM((STEPS, 2, halo, 2 * y_cols), jnp.float32),
            pltpu.VMEM((STEPS, 2, 8, rows), jnp.float32),
            pltpu.VMEM((STEPS, 2, 8, rows), jnp.float32),
            pltpu.SemaphoreType.DMA((STEPS, 4)),
            pltpu.SemaphoreType.DMA((STEPS, 4)),
            pltpu.SemaphoreType.DMA((devices,)),
            pltpu.SemaphoreType.DMA((devices,)),
            pltpu.SemaphoreType.DMA,
            pltpu.VMEM(slots.shape, jnp.float32),
            pltpu.SemaphoreType.DMA((z_depth,)),
            pltpu.SemaphoreType.DMA((z_depth,)),
            pltpu.SemaphoreType.DMA,
        ],
        compiler_params=pltpu.CompilerParams(
            collective_id=0, has_side_effects=True, vmem_limit_bytes=56 * 2**20
        ),
    )(model, u_prev, u_cur, a_next, a_cur, records, mass, *tables)


def halves(value):
    high = value.astype(jnp.bfloat16)
    return high, (value - high.astype(jnp.float32)).astype(jnp.bfloat16)


def dot_halves(left, right, right_dim=0):
    def product(a, b):
        return lax.dot_general(
            a, b, (((1,), (right_dim,)), ((), ())), preferred_element_type=jnp.float32
        )

    return product(left[0], right[0]) + (product(left[0], right[1]) + product(left[1], right[0]))


def spectral_kernel(
    grad_ref, mass_ref, x_high_ref, x_low_ref, y_high_ref, y_low_ref,
    out_ref,
    arrived, spectrum, y_high, y_low, back_high, back_low, leaving, partial,
    send_one, recv_one, send_two, recv_two, table_sem,
):
    chain = lax.axis_index("chain")
    tile = lax.axis_index("gx")
    devices = lax.axis_size("gx")
    planes, x_rows, y_cols = grad_ref.shape
    x_total = spectrum.shape[0]
    width = spectrum.shape[1] // 2
    plane, part = plane_and_part(tile, planes)

    loads = [
        pltpu.make_async_copy(y_high_ref.at[part], y_high, table_sem.at[0]),
        pltpu.make_async_copy(y_low_ref.at[part], y_low, table_sem.at[1]),
    ]
    for load in loads:
        load.start()
    barrier = pltpu.get_barrier_semaphore()

    @pl.loop(1, devices)
    def _(step):
        pl.semaphore_signal(
            barrier, inc=1, device_id=(chain, lax.rem(tile + step, devices)), device_id_type=MESH
        )

    def outward(step):
        peer = lax.rem(tile + step, devices)
        return pltpu.make_async_remote_copy(
            src_ref=grad_ref.at[plane_and_part(peer, planes)[0]],
            dst_ref=arrived.at[step],
            send_sem=send_one.at[step],
            recv_sem=recv_one.at[step],
            device_id=(chain, peer),
            device_id_type=MESH,
        )

    def homeward(step):
        return pltpu.make_async_remote_copy(
            src_ref=leaving.at[step],
            dst_ref=partial.at[step],
            send_sem=send_two.at[step],
            recv_sem=recv_two.at[step],
            device_id=(chain, lax.rem(tile + step, devices)),
            device_id_type=MESH,
        )

    spectrum[...] = jnp.zeros(spectrum.shape, jnp.float32)
    pl.semaphore_wait(barrier, devices - 1)

    @pl.loop(1, devices)
    def _(step):
        outward(step).start()

    for load in loads:
        load.wait()

    def block_rows(owner):
        return pl.ds(pl.multiple_of(owner // GY * x_rows, x_rows), x_rows)

    def table_rows(owner):
        return pl.ds(pl.multiple_of(lax.rem(owner, GY) * y_cols, y_cols), y_cols)

    def transform(owner, value):
        lines = table_rows(owner)
        spectrum[block_rows(owner), :] += dot_halves(
            halves(value), (y_high[lines, :], y_low[lines, :])
        )

    transform(tile, grad_ref[plane])

    @pl.loop(1, devices)
    def _(step):
        outward(step).wait_recv()
        transform(lax.rem(tile + devices - step, devices), arrived[step])

    def along_x(value, orient):
        mixed = dot_halves((x_high_ref[...], x_low_ref[...]), halves(value))
        cosine, sine = mixed[0:x_total], mixed[x_total:]
        real = cosine[:, 0:width] - orient * sine[:, width:]
        imag = cosine[:, width:] + orient * sine[:, 0:width]
        return real, imag

    real, imag = along_x(spectrum[...], -1.0)
    spectrum[:, 0:width] = real * mass_ref[...]
    spectrum[:, width:] = imag * mass_ref[...]
    real, imag = along_x(spectrum[...], 1.0)
    back_high[:, 0:width], back_low[:, 0:width] = halves(real)
    back_high[:, width:], back_low[:, width:] = halves(imag)

    def restored(owner):
        rows, lines = block_rows(owner), table_rows(owner)
        return dot_halves(
            (back_high[rows, :], back_low[rows, :]), (y_high[lines, :], y_low[lines, :]), 1
        )

    @pl.loop(1, devices)
    def _(step):
        leaving[step] = restored(lax.rem(tile + step, devices))
        homeward(step).start()

    out_ref[...] = jnp.zeros(out_ref.shape, jnp.float32)
    out_ref[plane] += restored(tile)

    @pl.loop(1, devices)
    def _(step):
        homeward(step).wait_recv()
        sender = lax.rem(tile + devices - step, devices)
        out_ref[plane_and_part(sender, planes)[0]] += partial[step]

    @pl.loop(1, devices)
    def _(step):
        outward(step).wait_send()
        homeward(step).wait_send()


def table_halves(table):
    high = table.astype(jnp.bfloat16)
    low = (table - high.astype(np.float64)).astype(jnp.bfloat16)
    return jnp.asarray(high), jnp.asarray(low)


def run_spectral(grad, mass):
    planes, x_rows, y_cols = grad.shape
    devices = lax.axis_size("gx")
    x_total, width = mass.shape
    y_total = y_cols * GY
    parts = y_total // width
    turn = np.arange(x_total)[:, None] * np.arange(x_total)[None, :] % x_total
    angle = turn * (2.0 * np.pi / x_total)
    x_tables = table_halves(np.concatenate((np.cos(angle), np.sin(angle)), axis=0))
    turn = np.arange(y_total)[:, None] * np.arange(y_total)[None, :] % y_total
    angle = (turn * (2.0 * np.pi / y_total)).reshape(y_total, parts, width).transpose(1, 0, 2)
    y_tables = table_halves(np.concatenate((np.cos(angle), -np.sin(angle)), axis=2))
    vmem = pl.BlockSpec(memory_space=pltpu.VMEM)
    hbm = pl.BlockSpec(memory_space=pl.ANY)
    tiles = (devices, x_rows, y_cols)
    return pl.pallas_call(
        spectral_kernel,
        out_shape=jax.ShapeDtypeStruct(grad.shape, jnp.float32),
        in_specs=[vmem] * 4 + [hbm] * 2,
        out_specs=vmem,
        scratch_shapes=[
            pltpu.VMEM(tiles, jnp.float32),
            pltpu.VMEM((x_total, 2 * width), jnp.float32),
            pltpu.VMEM((y_total, 2 * width), jnp.bfloat16),
            pltpu.VMEM((y_total, 2 * width), jnp.bfloat16),
            pltpu.VMEM((x_total, 2 * width), jnp.bfloat16),
            pltpu.VMEM((x_total, 2 * width), jnp.bfloat16),
            pltpu.VMEM(tiles, jnp.float32),
            pltpu.VMEM(tiles, jnp.float32),
            pltpu.SemaphoreType.DMA((devices,)),
            pltpu.SemaphoreType.DMA((devices,)),
            pltpu.SemaphoreType.DMA((devices,)),
            pltpu.SemaphoreType.DMA((devices,)),
            pltpu.SemaphoreType.DMA((2,)),
        ],
        compiler_params=pltpu.CompilerParams(
            collective_id=1, has_side_effects=True, vmem_limit_bytes=48 * 2**20
        ),
    )(grad, mass, *x_tables, *y_tables)


def pick_factor(length):
    candidate = math.isqrt(length)
    if candidate * candidate < length:
        candidate = candidate + 1
    while length % candidate != 0:
        candidate = candidate + 1
    return candidate


def phase_tables(rows_count, cols_count, modulus):
    first = jnp.arange(rows_count, dtype=jnp.int32)
    second = jnp.arange(cols_count, dtype=jnp.int32)
    phase_int = first[:, None] * second[None, :] % modulus
    angle_rad = phase_int.astype(jnp.float32) * (2.0 * math.pi / modulus)
    return (jnp.cos(angle_rad), jnp.sin(angle_rad))


def complex_mix(form, tab_cos, tab_sin, real_part, imag_part, orient):

    def product(table, data):
        return jnp.einsum(
            form, table, data, precision=lax.Precision.HIGHEST, preferred_element_type=jnp.float32
        )

    out_real = product(tab_cos, real_part) - orient * product(tab_sin, imag_part)
    out_imag = product(tab_cos, imag_part) + orient * product(tab_sin, real_part)
    return (out_real, out_imag)


def transform_rows(real_part, imag_part, orient):
    length, width = real_part.shape
    outer_len = pick_factor(length)
    inner_len = length // outer_len
    data_re = real_part.reshape(outer_len, inner_len, width)
    data_im = imag_part.reshape(outer_len, inner_len, width)
    cos_outer, sin_outer = phase_tables(outer_len, outer_len, outer_len)
    mid_re, mid_im = complex_mix("ca,abm->cbm", cos_outer, sin_outer, data_re, data_im, orient)
    twist_cos, twist_sin = phase_tables(outer_len, inner_len, length)
    twist_cos = twist_cos[:, :, None]
    twist_sin = twist_sin[:, :, None]
    turned_re = mid_re * twist_cos - orient * mid_im * twist_sin
    turned_im = mid_im * twist_cos + orient * mid_re * twist_sin
    cos_inner, sin_inner = phase_tables(inner_len, inner_len, inner_len)
    final_re, final_im = complex_mix(
        "db,cbm->dcm", cos_inner, sin_inner, turned_re, turned_im, orient
    )
    return (final_re.reshape(length, width), final_im.reshape(length, width))


def per_device(
    courant, ckpt_prev, ckpt_cur, adj_next, adj_cur, rec_x, rec_plane, traces, mass_kernel
):
    x_rows, z_depth, y_cols = courant.shape[1:]
    devices = lax.axis_size("gx")
    x_blocks = devices // GY
    x_total = x_rows * x_blocks
    y_total = y_cols * GY
    cell_y = rec_plane % y_total
    cell_z = rec_plane // y_total
    owner = rec_x // x_rows * GY + cell_y // y_cols
    cell_row = (owner * x_rows + rec_x % x_rows) * z_depth + cell_z
    records = jnp.concatenate(
        (
            cell_row.astype(jnp.float32)[None],
            (cell_y % y_cols).astype(jnp.float32)[None],
            traces,
            jnp.zeros((6 - STEPS, rec_x.shape[0]), jnp.float32),
        ),
        axis=0,
    )
    dense = x_total <= 512 and GY % z_depth == 0 and devices % z_depth == 0
    mass = mass_kernel.reshape(-1, 128) if dense else jnp.zeros((8, 128), jnp.float32)
    gradient, adj_now, adj_later, mass_slots = run_window(
        *(
            field.reshape(x_rows * z_depth, y_cols)
            for field in (courant, ckpt_prev, ckpt_cur, adj_next, adj_cur)
        ),
        records,
        mass,
        dense,
    )
    tile_shape = (1, x_rows, z_depth, y_cols)
    if dense:
        by_plane = gradient.reshape(x_rows, z_depth, y_cols).transpose(1, 0, 2)
        part_mass = mass_slots.reshape(z_depth, x_total, -1).transpose(1, 0, 2)
        part_mass = part_mass.reshape(x_total, -1) * (1.0 / (x_total * y_total))
        scaled = run_spectral(by_plane, part_mass).transpose(1, 0, 2)
        return (
            scaled.reshape(tile_shape),
            adj_now.reshape(tile_shape),
            adj_later.reshape(tile_shape),
        )
    flat_grad = gradient.reshape(x_rows * z_depth, 1, y_cols)
    rows = lax.all_to_all(flat_grad, "gx", split_axis=0, concat_axis=1, tiled=True)
    share = rows.shape[0]
    lines = rows.reshape(share * x_blocks, y_total).T
    spec_re_t, spec_im_t = transform_rows(lines, jnp.zeros_like(lines), -1.0)
    spec_re = spec_re_t.T.reshape(share, x_blocks, y_total)
    spec_im = spec_im_t.T.reshape(share, x_blocks, y_total)
    cols_re, cols_im = (
        lax.all_to_all(spec_re, "gx", split_axis=2, concat_axis=0, tiled=True),
        lax.all_to_all(spec_im, "gx", split_axis=2, concat_axis=0, tiled=True),
    )
    col_width = cols_re.shape[2]
    half_width = z_depth * col_width

    def to_columns(part):
        return (
            part.reshape(x_rows, z_depth, x_blocks, col_width)
            .transpose(2, 0, 1, 3)
            .reshape(x_total, half_width)
        )

    def from_columns(part):
        return (
            part.reshape(x_blocks, x_rows, z_depth, col_width)
            .transpose(1, 2, 0, 3)
            .reshape(devices * share, x_blocks, col_width)
        )

    freq_re, freq_im = transform_rows(to_columns(cols_re), to_columns(cols_im), -1.0)
    kernel_scale = (
        jnp.broadcast_to(mass_kernel[:, None, :], (x_total, z_depth, col_width)).reshape(
            x_total, half_width
        )
        / x_total
    )
    freq_re = freq_re * kernel_scale
    freq_im = freq_im * kernel_scale
    spat_re, spat_im = transform_rows(freq_re, freq_im, 1.0)
    back_re = from_columns(spat_re)
    back_im = from_columns(spat_im)
    line_re, line_im = (
        lax.all_to_all(back_re, "gx", split_axis=0, concat_axis=2, tiled=True),
        lax.all_to_all(back_im, "gx", split_axis=0, concat_axis=2, tiled=True),
    )
    lines_re = line_re.reshape(share * x_blocks, y_total).T
    lines_im = line_im.reshape(share * x_blocks, y_total).T
    real_t, imag_t = transform_rows(lines_re, lines_im, 1.0)
    real_lines = (real_t.T / y_total).reshape(share, devices, y_cols)
    tiled = lax.all_to_all(real_lines, "gx", split_axis=1, concat_axis=0, tiled=True)
    return (tiled.reshape(tile_shape), adj_now.reshape(tile_shape), adj_later.reshape(tile_shape))


def solution(mesh):
    in_specs = (
        P(("chain", "gx"), None, None, None),
        P(("chain", "gx"), None, None, None),
        P(("chain", "gx"), None, None, None),
        P(("chain", "gx"), None, None, None),
        P(("chain", "gx"), None, None, None),
        P(("chain", "gx")),
        P(("chain", "gx")),
        P(None, ("chain", "gx")),
        P(None, "gx"),
    )
    out_specs = (
        P(("chain", "gx"), None, None, None),
        P(("chain", "gx"), None, None, None),
        P(("chain", "gx"), None, None, None),
    )
    return jax.shard_map(
        per_device, mesh=mesh, in_specs=in_specs, out_specs=out_specs, check_vma=False
    )
```

```python
import functools
import math

import jax
import jax.numpy as jnp
import numpy as np
from jax import lax
from jax.experimental import pallas as pl
from jax.experimental.pallas import tpu as pltpu
from jax.sharding import PartitionSpec as P

GY = 8
STEPS = 4


STENCIL_COEF = (-205.0 / 72.0, 8.0 / 5.0, -1.0 / 5.0, 8.0 / 315.0, -1.0 / 560.0)


MESH = pl.DeviceIdType.MESH
HIGHEST = lax.Precision.HIGHEST


def dot_f32(left, right, left_dim=1, right_dim=0):
    return lax.dot_general(
        left,
        right,
        (((left_dim,), (right_dim,)), ((), ())),
        precision=HIGHEST,
        preferred_element_type=jnp.float32,
    )


def stencil_tables(z_depth, y_cols, chunk):
    coef = np.array(STENCIL_COEF, np.float64)
    halo = 4 * z_depth
    row = np.arange(chunk)[:, None]
    col = np.arange(chunk + 2 * halo)[None, :] - halo
    dx = np.abs(row // z_depth - col // z_depth)
    dz = np.abs(row % z_depth - col % z_depth)
    band = np.where((dz == 0) & (dx <= 4), coef[np.minimum(dx, 4)], 0.0)
    band = band + np.where((dx == 0) & (dz <= 4), coef[np.minimum(dz, 4)], 0.0)
    lane = np.arange(y_cols)
    dy = np.abs(lane[:, None] - lane[None, :])
    along_y = np.where(dy <= 4, coef[np.minimum(dy, 4)], 0.0)
    along_y = np.kron(np.eye(2), along_y)
    edge = np.arange(halo)
    near = edge[:, None] // z_depth + 4 - edge[None, :] // z_depth
    same = edge[:, None] % z_depth == edge[None, :] % z_depth
    from_low = np.where(same & (near <= 4), coef[np.minimum(near, 4)], 0.0)
    far = 4 + edge[None, :] // z_depth - edge[:, None] // z_depth
    from_high = np.where(same & (far <= 4), coef[np.minimum(far, 4)], 0.0)
    rim = np.zeros((16, 2 * y_cols))
    for field in range(2):
        for depth in range(4):
            for y in range(4):
                if y + 4 - depth <= 4:
                    rim[field * 4 + depth, field * y_cols + y] = coef[y + 4 - depth]
                last = y_cols - 1 - y
                gap = y_cols + depth - last
                if gap <= 4:
                    rim[8 + field * 4 + depth, field * y_cols + last] = coef[gap]
    pick = np.zeros((16, 2 * y_cols))
    for field in range(2):
        for depth in range(4):
            pick[field * 4 + depth, field * y_cols + depth] = 1.0
            pick[8 + field * 4 + depth, field * y_cols + y_cols - 4 + depth] = 1.0
    tables = (band, along_y, from_low, from_high, rim, pick)
    return [jnp.asarray(table.astype(np.float32)) for table in tables]


def plane_and_part(tile, planes):
    share = GY // planes
    column = lax.rem(tile, GY)
    return column // share, tile // GY * share + lax.rem(column, share)


def plane_holder(plane, part, planes):
    share = GY // planes
    return part // share * GY + plane * share + lax.rem(part, share)


def window_kernel(
    chunk, move_mass,
    model_ref, prev_ref, cur_ref, next_ref, now_ref, rec_ref, mass_ref,
    band_ref, along_ref, low_ref, high_ref, rim_ref, pick_ref,
    grad_ref, first_ref, second_ref, mass_out,
    both, lap, images, waves, adjoints, records, hot, weights, inject,
    x_out, x_in, y_out, y_in, halo_send, halo_recv, rec_send, rec_recv, own_sem,
    mass_in, mass_send, mass_recv, mass_own,
):
    chain = lax.axis_index("chain")
    tile = lax.axis_index("gx")
    devices = lax.axis_size("gx")
    x_blocks = devices // GY
    rows, y_cols = model_ref.shape
    halo = x_out.shape[2]
    column = lax.rem(tile, GY)
    block = tile // GY
    neighbours = (
        lax.rem(block + x_blocks - 1, x_blocks) * GY + column,
        lax.rem(block + 1, x_blocks) * GY + column,
        block * GY + lax.rem(column + GY - 1, GY),
        block * GY + lax.rem(column + 1, GY),
    )
    has_low = (block > 0).astype(jnp.float32)
    has_high = (block < x_blocks - 1).astype(jnp.float32)
    has_left = (column > 0).astype(jnp.float32)
    has_right = (column < GY - 1).astype(jnp.float32)

    own = pltpu.make_async_copy(rec_ref, records.at[0], own_sem)
    own.start()
    barrier = pltpu.get_barrier_semaphore()

    @pl.loop(1, devices)
    def _(step):
        pl.semaphore_signal(
            barrier, inc=1, device_id=(chain, lax.rem(tile + step, devices)), device_id_type=MESH
        )

    both[0:halo, :] = jnp.zeros((halo, 2 * y_cols), jnp.float32)
    both[halo + rows :, :] = jnp.zeros((halo, 2 * y_cols), jnp.float32)
    low_rows = lax.broadcasted_iota(jnp.int32, rim_ref.shape, 0) < 8
    rim = rim_ref[...] * jnp.where(low_rows, has_left, has_right)

    along = halves(along_ref[...])
    band = halves(band_ref[...])

    def pack(phase, wave, adjoint):
        both[halo : halo + rows, 0:y_cols] = wave
        both[halo : halo + rows, y_cols:] = model_ref[...] * adjoint
        x_out[phase, 0] = both[halo : 2 * halo, :]
        x_out[phase, 1] = both[rows : halo + rows, :]
        strips = dot_f32(pick_ref[...], both[halo : halo + rows, :], 1, 1)
        y_out[phase, 0] = strips[0:8]
        y_out[phase, 1] = strips[8:16]

    def halo_copies(phase):
        copies = []
        for way in range(4):
            source = x_out if way < 2 else y_out
            target = x_in if way < 2 else y_in
            copies.append(
                pltpu.make_async_remote_copy(
                    src_ref=source.at[phase, way % 2],
                    dst_ref=target.at[phase, 1 - way % 2],
                    send_sem=halo_send.at[phase, way],
                    recv_sem=halo_recv.at[phase, way],
                    device_id=(chain, neighbours[way]),
                    device_id_type=MESH,
                )
            )
        return copies

    def record_copy(step):
        return pltpu.make_async_remote_copy(
            src_ref=rec_ref,
            dst_ref=records.at[step],
            send_sem=rec_send.at[step],
            recv_sem=rec_recv.at[step],
            device_id=(chain, lax.rem(tile + step, devices)),
            device_id_type=MESH,
        )

    slots = mass_in.shape[0]
    _, quarter = plane_and_part(tile, slots)

    def mass_copies(number):
        target = plane_holder(number, tile // slots, slots)
        remote = pltpu.make_async_remote_copy(
            src_ref=mass_ref,
            dst_ref=mass_in.at[lax.rem(tile, slots)],
            send_sem=mass_send.at[number],
            recv_sem=mass_recv.at[lax.rem(tile, slots)],
            device_id=(chain, target),
            device_id_type=MESH,
        )
        local = pltpu.make_async_copy(mass_ref, mass_in.at[lax.rem(tile, slots)], mass_own)
        return target != tile, remote, local

    def mass_start():
        for number in range(slots):
            away, remote, local = mass_copies(number)
            pl.when(away)(remote.start)
            pl.when(jnp.logical_not(away))(local.start)

    def mass_finish():
        for number in range(slots):
            away, remote, local = mass_copies(number)
            pl.when(away)(remote.wait_send)
            pl.when(jnp.logical_not(away))(local.wait)
        for slot in range(slots):
            arrival = pltpu.make_async_remote_copy(
                src_ref=mass_ref,
                dst_ref=mass_in.at[slot],
                send_sem=mass_send.at[slot],
                recv_sem=mass_recv.at[slot],
                device_id=(chain, lax.rem(tile + 1, devices)),
                device_id_type=MESH,
            )
            pl.when(quarter * slots + slot != tile)(arrival.wait_recv)
        mass_out[...] = mass_in[...]

    pack(0, cur_ref[...], now_ref[...])
    pl.semaphore_wait(barrier, devices - 1)
    pending = []
    width = rec_ref.shape[1]
    total = devices * width
    part = math.gcd(total, 2048)
    for phase in range(STEPS):
        copies = halo_copies(phase)
        for copy in copies:
            copy.start()
        pending += copies
        if phase == 0:

            @pl.loop(1, devices)
            def _(step):
                record_copy(step).start()

            if move_mass:
                mass_start()

        high, low = halves(both[...])
        for start in range(0, rows, chunk):
            inner = slice(halo + start, halo + start + chunk)
            outer = slice(start, start + chunk + 2 * halo)
            lap[start : start + chunk, :] = dot_halves(
                (high[inner], low[inner]), along
            ) + dot_halves(band, (high[outer], low[outer]))
        if phase == 0:
            own.wait()

            @pl.loop(1, devices)
            def _(step):
                record_copy(step).wait()

            @pl.loop(0, devices)
            def _(step):
                lanes = pl.ds(pl.multiple_of(step * width, width), width)
                cell = records[step, 0:1, :] - (tile * rows).astype(jnp.float32)
                index = lax.broadcasted_iota(jnp.int32, (rows, width), 0).astype(jnp.float32)
                hot[:, lanes] = jnp.where(index == cell, 1.0, 0.0).astype(jnp.bfloat16)

        section = STEPS - 1 - phase

        @pl.loop(0, devices)
        def _(step):
            lanes = pl.ds(pl.multiple_of(step * width, width), width)
            place = records[step, 1:2, :]
            value = records[step, 2 + section : 3 + section, :]
            index = lax.broadcasted_iota(jnp.int32, (y_cols, width), 0).astype(jnp.float32)
            rest = jnp.where(index == place, value, 0.0)
            for level in range(2):
                piece = rest.astype(jnp.bfloat16)
                weights[level * y_cols : (level + 1) * y_cols, lanes] = piece
                rest = rest - piece.astype(jnp.float32)

        def injected(lanes):
            pair = lax.dot_general(
                hot[:, lanes],
                weights[:, lanes],
                (((1,), (1,)), ((), ())),
                preferred_element_type=jnp.float32,
            )
            return pair[:, 0:y_cols] + pair[:, y_cols:]

        inject[...] = injected(pl.ds(0, part))
        if total > part:

            @pl.loop(1, total // part)
            def _(step):
                inject[...] += injected(pl.ds(pl.multiple_of(step * part, part), part))

        for copy in copies:
            copy.wait_recv()
        sides = jnp.concatenate((y_in[phase, 0], y_in[phase, 1]), axis=0)
        lap[...] += dot_f32(sides, rim, 0, 0)
        lap[0:halo, :] += has_low * dot_f32(low_ref[...], x_in[phase, 0])
        lap[rows - halo :, :] += has_high * dot_f32(high_ref[...], x_in[phase, 1])
        image = lap[:, 0:y_cols]
        images[phase] = image
        if phase + 1 < STEPS:
            older = prev_ref[...] if phase == 0 else (cur_ref[...] if phase == 1 else waves[0])
            newer = cur_ref[...] if phase == 0 else waves[phase - 1]
            waves[phase] = 2.0 * newer - older + model_ref[...] * image
        later = next_ref[...] if phase == 0 else (now_ref[...] if phase == 1 else adjoints[phase - 2])
        now = now_ref[...] if phase == 0 else adjoints[phase - 1]
        adjoints[phase] = 2.0 * now - later + lap[:, y_cols:] + inject[...]
        if phase + 1 < STEPS:
            pack(phase + 1, waves[phase], adjoints[phase])
    grad_ref[...] = (
        now_ref[...] * images[3]
        + adjoints[0] * images[2]
        + adjoints[1] * images[1]
        + adjoints[2] * images[0]
    )
    first_ref[...] = adjoints[3]
    second_ref[...] = adjoints[2]
    for copy in pending:
        copy.wait_send()
    if move_mass:
        mass_finish()
    else:
        mass_out[...] = jnp.zeros(mass_out.shape, jnp.float32)


def run_window(model, u_prev, u_cur, a_next, a_cur, records, mass, move_mass):
    rows, y_cols = model.shape
    z_depth = 4
    devices = lax.axis_size("gx")
    halo = 4 * z_depth
    chunk = 128
    total = devices * records.shape[1]
    tables = stencil_tables(z_depth, y_cols, chunk)
    field = jax.ShapeDtypeStruct((rows, y_cols), jnp.float32)
    slots = jax.ShapeDtypeStruct((z_depth,) + mass.shape, jnp.float32)
    vmem = pl.BlockSpec(memory_space=pltpu.VMEM)
    return pl.pallas_call(
        functools.partial(window_kernel, chunk, move_mass),
        out_shape=(field, field, field, slots),
        in_specs=[vmem] * 13,
        out_specs=(vmem,) * 4,
        scratch_shapes=[
            pltpu.VMEM((rows + 2 * halo, 2 * y_cols), jnp.float32),
            pltpu.VMEM((rows, 2 * y_cols), jnp.float32),
            pltpu.VMEM((STEPS, rows, y_cols), jnp.float32),
            pltpu.VMEM((STEPS - 1, rows, y_cols), jnp.float32),
            pltpu.VMEM((STEPS, rows, y_cols), jnp.float32),
            pltpu.VMEM((devices,) + records.shape, jnp.float32),
            pltpu.VMEM((rows, total), jnp.bfloat16),
            pltpu.VMEM((2 * y_cols, total), jnp.bfloat16),
            pltpu.VMEM((rows, y_cols), jnp.float32),
            pltpu.VMEM((STEPS, 2, halo, 2 * y_cols), jnp.float32),
            pltpu.VMEM((STEPS, 2, halo, 2 * y_cols), jnp.float32),
            pltpu.VMEM((STEPS, 2, 8, rows), jnp.float32),
            pltpu.VMEM((STEPS, 2, 8, rows), jnp.float32),
            pltpu.SemaphoreType.DMA((STEPS, 4)),
            pltpu.SemaphoreType.DMA((STEPS, 4)),
            pltpu.SemaphoreType.DMA((devices,)),
            pltpu.SemaphoreType.DMA((devices,)),
            pltpu.SemaphoreType.DMA,
            pltpu.VMEM(slots.shape, jnp.float32),
            pltpu.SemaphoreType.DMA((z_depth,)),
            pltpu.SemaphoreType.DMA((z_depth,)),
            pltpu.SemaphoreType.DMA,
        ],
        compiler_params=pltpu.CompilerParams(
            collective_id=0, has_side_effects=True, vmem_limit_bytes=56 * 2**20
        ),
    )(model, u_prev, u_cur, a_next, a_cur, records, mass, *tables)


def halves(value):
    high = value.astype(jnp.bfloat16)
    return high, (value - high.astype(jnp.float32)).astype(jnp.bfloat16)


def dot_halves(left, right, right_dim=0):
    def product(a, b):
        return lax.dot_general(
            a, b, (((1,), (right_dim,)), ((), ())), preferred_element_type=jnp.float32
        )

    return product(left[0], right[0]) + (product(left[0], right[1]) + product(left[1], right[0]))


def spectral_kernel(
    grad_ref, mass_ref, x_high_ref, x_low_ref, y_high_ref, y_low_ref,
    out_ref,
    arrived, spectrum, y_high, y_low, back_high, back_low, leaving, partial,
    send_one, recv_one, send_two, recv_two, table_sem,
):
    chain = lax.axis_index("chain")
    tile = lax.axis_index("gx")
    devices = lax.axis_size("gx")
    planes, x_rows, y_cols = grad_ref.shape
    x_total = spectrum.shape[0]
    width = spectrum.shape[1] // 2
    plane, part = plane_and_part(tile, planes)

    loads = [
        pltpu.make_async_copy(y_high_ref.at[part], y_high, table_sem.at[0]),
        pltpu.make_async_copy(y_low_ref.at[part], y_low, table_sem.at[1]),
    ]
    for load in loads:
        load.start()
    barrier = pltpu.get_barrier_semaphore()

    @pl.loop(1, devices)
    def _(step):
        pl.semaphore_signal(
            barrier, inc=1, device_id=(chain, lax.rem(tile + step, devices)), device_id_type=MESH
        )

    sibling = tile + 1 - 2 * lax.rem(tile, 2)
    turns = devices // 2

    def copy_to(peer, source, target, send_sem, recv_sem):
        return pltpu.make_async_remote_copy(
            src_ref=source,
            dst_ref=target,
            send_sem=send_sem,
            recv_sem=recv_sem,
            device_id=(chain, peer),
            device_id_type=MESH,
        )

    def ahead(first, turn):
        return lax.rem(first + 2 * turn, devices)

    def behind(first, turn):
        return lax.rem(first + devices - 2 * turn, devices)

    def outward(turn):
        peer = ahead(tile, turn)
        slot = 2 * turn
        source = grad_ref.at[plane_and_part(peer, planes)[0]]
        return copy_to(peer, source, arrived.at[slot], send_one.at[slot], recv_one.at[slot])

    def forward(turn):
        slot = 2 * turn + 1
        return copy_to(
            sibling, arrived.at[2 * turn], arrived.at[slot], send_one.at[slot], recv_one.at[slot]
        )

    def homeward(turn):
        slot = 2 * turn
        return copy_to(
            ahead(tile, turn), leaving.at[slot], partial.at[slot], send_two.at[slot], recv_two.at[slot]
        )

    def across(turn):
        slot = 2 * turn + 1
        return copy_to(
            sibling, leaving.at[slot], partial.at[slot], send_two.at[slot], recv_two.at[slot]
        )

    spectrum[...] = jnp.zeros(spectrum.shape, jnp.float32)
    pl.semaphore_wait(barrier, devices - 1)

    @pl.loop(1, turns)
    def _(turn):
        outward(turn).start()

    arrived[0] = grad_ref[plane]
    forward(0).start()
    for load in loads:
        load.wait()

    def block_rows(owner):
        return pl.ds(pl.multiple_of(owner // GY * x_rows, x_rows), x_rows)

    def table_rows(owner):
        return pl.ds(pl.multiple_of(lax.rem(owner, GY) * y_cols, y_cols), y_cols)

    def transform(owner, value):
        lines = table_rows(owner)
        spectrum[block_rows(owner), :] += dot_halves(
            halves(value), (y_high[lines, :], y_low[lines, :])
        )

    transform(tile, grad_ref[plane])

    def take_forwarded(turn):
        forward(turn).wait_recv()
        transform(behind(sibling, turn), arrived[2 * turn + 1])

    @pl.loop(1, turns)
    def _(turn):
        outward(turn).wait_recv()
        forward(turn).start()
        transform(behind(tile, turn), arrived[2 * turn])
        take_forwarded(turn - 1)

    take_forwarded(turns - 1)

    def along_x(value, orient):
        mixed = dot_halves((x_high_ref[...], x_low_ref[...]), halves(value))
        cosine, sine = mixed[0:x_total], mixed[x_total:]
        real = cosine[:, 0:width] - orient * sine[:, width:]
        imag = cosine[:, width:] + orient * sine[:, 0:width]
        return real, imag

    real, imag = along_x(spectrum[...], -1.0)
    spectrum[:, 0:width] = real * mass_ref[...]
    spectrum[:, width:] = imag * mass_ref[...]
    real, imag = along_x(spectrum[...], 1.0)
    back_high[:, 0:width], back_low[:, 0:width] = halves(real)
    back_high[:, width:], back_low[:, width:] = halves(imag)

    def restored(owner):
        rows, lines = block_rows(owner), table_rows(owner)
        return dot_halves(
            (back_high[rows, :], back_low[rows, :]), (y_high[lines, :], y_low[lines, :]), 1
        )

    def pass_across(turn):
        leaving[2 * turn + 1] = restored(ahead(sibling, turn))
        across(turn).start()

    pass_across(1)

    @pl.loop(1, turns)
    def _(turn):
        pass_across(lax.rem(turn + 1, turns))
        own = restored(ahead(tile, turn))
        across(turn).wait_recv()
        leaving[2 * turn] = own + partial[2 * turn + 1]
        homeward(turn).start()

    out_ref[...] = jnp.zeros(out_ref.shape, jnp.float32)
    mine = restored(tile)
    across(0).wait_recv()
    out_ref[plane] += mine + partial[1]

    @pl.loop(1, turns)
    def _(turn):
        homeward(turn).wait_recv()
        out_ref[plane_and_part(behind(tile, turn), planes)[0]] += partial[2 * turn]

    forward(0).wait_send()
    across(0).wait_send()

    @pl.loop(1, turns)
    def _(turn):
        outward(turn).wait_send()
        forward(turn).wait_send()
        across(turn).wait_send()
        homeward(turn).wait_send()


def table_halves(table):
    high = table.astype(jnp.bfloat16)
    low = (table - high.astype(np.float64)).astype(jnp.bfloat16)
    return jnp.asarray(high), jnp.asarray(low)


def run_spectral(grad, mass):
    planes, x_rows, y_cols = grad.shape
    devices = lax.axis_size("gx")
    x_total, width = mass.shape
    y_total = y_cols * GY
    parts = y_total // width
    turn = np.arange(x_total)[:, None] * np.arange(x_total)[None, :] % x_total
    angle = turn * (2.0 * np.pi / x_total)
    x_tables = table_halves(np.concatenate((np.cos(angle), np.sin(angle)), axis=0))
    turn = np.arange(y_total)[:, None] * np.arange(y_total)[None, :] % y_total
    angle = (turn * (2.0 * np.pi / y_total)).reshape(y_total, parts, width).transpose(1, 0, 2)
    y_tables = table_halves(np.concatenate((np.cos(angle), -np.sin(angle)), axis=2))
    vmem = pl.BlockSpec(memory_space=pltpu.VMEM)
    hbm = pl.BlockSpec(memory_space=pl.ANY)
    tiles = (devices, x_rows, y_cols)
    return pl.pallas_call(
        spectral_kernel,
        out_shape=jax.ShapeDtypeStruct(grad.shape, jnp.float32),
        in_specs=[vmem] * 4 + [hbm] * 2,
        out_specs=vmem,
        scratch_shapes=[
            pltpu.VMEM(tiles, jnp.float32),
            pltpu.VMEM((x_total, 2 * width), jnp.float32),
            pltpu.VMEM((y_total, 2 * width), jnp.bfloat16),
            pltpu.VMEM((y_total, 2 * width), jnp.bfloat16),
            pltpu.VMEM((x_total, 2 * width), jnp.bfloat16),
            pltpu.VMEM((x_total, 2 * width), jnp.bfloat16),
            pltpu.VMEM(tiles, jnp.float32),
            pltpu.VMEM(tiles, jnp.float32),
            pltpu.SemaphoreType.DMA((devices,)),
            pltpu.SemaphoreType.DMA((devices,)),
            pltpu.SemaphoreType.DMA((devices,)),
            pltpu.SemaphoreType.DMA((devices,)),
            pltpu.SemaphoreType.DMA((2,)),
        ],
        compiler_params=pltpu.CompilerParams(
            collective_id=1, has_side_effects=True, vmem_limit_bytes=48 * 2**20
        ),
    )(grad, mass, *x_tables, *y_tables)


def pick_factor(length):
    candidate = math.isqrt(length)
    if candidate * candidate < length:
        candidate = candidate + 1
    while length % candidate != 0:
        candidate = candidate + 1
    return candidate


def phase_tables(rows_count, cols_count, modulus):
    first = jnp.arange(rows_count, dtype=jnp.int32)
    second = jnp.arange(cols_count, dtype=jnp.int32)
    phase_int = first[:, None] * second[None, :] % modulus
    angle_rad = phase_int.astype(jnp.float32) * (2.0 * math.pi / modulus)
    return (jnp.cos(angle_rad), jnp.sin(angle_rad))


def complex_mix(form, tab_cos, tab_sin, real_part, imag_part, orient):

    def product(table, data):
        return jnp.einsum(
            form, table, data, precision=lax.Precision.HIGHEST, preferred_element_type=jnp.float32
        )

    out_real = product(tab_cos, real_part) - orient * product(tab_sin, imag_part)
    out_imag = product(tab_cos, imag_part) + orient * product(tab_sin, real_part)
    return (out_real, out_imag)


def transform_rows(real_part, imag_part, orient):
    length, width = real_part.shape
    outer_len = pick_factor(length)
    inner_len = length // outer_len
    data_re = real_part.reshape(outer_len, inner_len, width)
    data_im = imag_part.reshape(outer_len, inner_len, width)
    cos_outer, sin_outer = phase_tables(outer_len, outer_len, outer_len)
    mid_re, mid_im = complex_mix("ca,abm->cbm", cos_outer, sin_outer, data_re, data_im, orient)
    twist_cos, twist_sin = phase_tables(outer_len, inner_len, length)
    twist_cos = twist_cos[:, :, None]
    twist_sin = twist_sin[:, :, None]
    turned_re = mid_re * twist_cos - orient * mid_im * twist_sin
    turned_im = mid_im * twist_cos + orient * mid_re * twist_sin
    cos_inner, sin_inner = phase_tables(inner_len, inner_len, inner_len)
    final_re, final_im = complex_mix(
        "db,cbm->dcm", cos_inner, sin_inner, turned_re, turned_im, orient
    )
    return (final_re.reshape(length, width), final_im.reshape(length, width))


def per_device(
    courant, ckpt_prev, ckpt_cur, adj_next, adj_cur, rec_x, rec_plane, traces, mass_kernel
):
    x_rows, z_depth, y_cols = courant.shape[1:]
    devices = lax.axis_size("gx")
    x_blocks = devices // GY
    x_total = x_rows * x_blocks
    y_total = y_cols * GY
    cell_y = rec_plane % y_total
    cell_z = rec_plane // y_total
    owner = rec_x // x_rows * GY + cell_y // y_cols
    cell_row = (owner * x_rows + rec_x % x_rows) * z_depth + cell_z
    records = jnp.concatenate(
        (
            cell_row.astype(jnp.float32)[None],
            (cell_y % y_cols).astype(jnp.float32)[None],
            traces,
            jnp.zeros((6 - STEPS, rec_x.shape[0]), jnp.float32),
        ),
        axis=0,
    )
    dense = x_total <= 512 and GY == 2 * z_depth and devices % z_depth == 0
    mass = mass_kernel.reshape(-1, 128) if dense else jnp.zeros((8, 128), jnp.float32)
    gradient, adj_now, adj_later, mass_slots = run_window(
        *(
            field.reshape(x_rows * z_depth, y_cols)
            for field in (courant, ckpt_prev, ckpt_cur, adj_next, adj_cur)
        ),
        records,
        mass,
        dense,
    )
    tile_shape = (1, x_rows, z_depth, y_cols)
    if dense:
        by_plane = gradient.reshape(x_rows, z_depth, y_cols).transpose(1, 0, 2)
        part_mass = mass_slots.reshape(z_depth, x_total, -1).transpose(1, 0, 2)
        part_mass = part_mass.reshape(x_total, -1) * (1.0 / (x_total * y_total))
        scaled = run_spectral(by_plane, part_mass).transpose(1, 0, 2)
        return (
            scaled.reshape(tile_shape),
            adj_now.reshape(tile_shape),
            adj_later.reshape(tile_shape),
        )
    flat_grad = gradient.reshape(x_rows * z_depth, 1, y_cols)
    rows = lax.all_to_all(flat_grad, "gx", split_axis=0, concat_axis=1, tiled=True)
    share = rows.shape[0]
    lines = rows.reshape(share * x_blocks, y_total).T
    spec_re_t, spec_im_t = transform_rows(lines, jnp.zeros_like(lines), -1.0)
    spec_re = spec_re_t.T.reshape(share, x_blocks, y_total)
    spec_im = spec_im_t.T.reshape(share, x_blocks, y_total)
    cols_re, cols_im = (
        lax.all_to_all(spec_re, "gx", split_axis=2, concat_axis=0, tiled=True),
        lax.all_to_all(spec_im, "gx", split_axis=2, concat_axis=0, tiled=True),
    )
    col_width = cols_re.shape[2]
    half_width = z_depth * col_width

    def to_columns(part):
        return (
            part.reshape(x_rows, z_depth, x_blocks, col_width)
            .transpose(2, 0, 1, 3)
            .reshape(x_total, half_width)
        )

    def from_columns(part):
        return (
            part.reshape(x_blocks, x_rows, z_depth, col_width)
            .transpose(1, 2, 0, 3)
            .reshape(devices * share, x_blocks, col_width)
        )

    freq_re, freq_im = transform_rows(to_columns(cols_re), to_columns(cols_im), -1.0)
    kernel_scale = (
        jnp.broadcast_to(mass_kernel[:, None, :], (x_total, z_depth, col_width)).reshape(
            x_total, half_width
        )
        / x_total
    )
    freq_re = freq_re * kernel_scale
    freq_im = freq_im * kernel_scale
    spat_re, spat_im = transform_rows(freq_re, freq_im, 1.0)
    back_re = from_columns(spat_re)
    back_im = from_columns(spat_im)
    line_re, line_im = (
        lax.all_to_all(back_re, "gx", split_axis=0, concat_axis=2, tiled=True),
        lax.all_to_all(back_im, "gx", split_axis=0, concat_axis=2, tiled=True),
    )
    lines_re = line_re.reshape(share * x_blocks, y_total).T
    lines_im = line_im.reshape(share * x_blocks, y_total).T
    real_t, imag_t = transform_rows(lines_re, lines_im, 1.0)
    real_lines = (real_t.T / y_total).reshape(share, devices, y_cols)
    tiled = lax.all_to_all(real_lines, "gx", split_axis=1, concat_axis=0, tiled=True)
    return (tiled.reshape(tile_shape), adj_now.reshape(tile_shape), adj_later.reshape(tile_shape))


def solution(mesh):
    in_specs = (
        P(("chain", "gx"), None, None, None),
        P(("chain", "gx"), None, None, None),
        P(("chain", "gx"), None, None, None),
        P(("chain", "gx"), None, None, None),
        P(("chain", "gx"), None, None, None),
        P(("chain", "gx")),
        P(("chain", "gx")),
        P(None, ("chain", "gx")),
        P(None, "gx"),
    )
    out_specs = (
        P(("chain", "gx"), None, None, None),
        P(("chain", "gx"), None, None, None),
        P(("chain", "gx"), None, None, None),
    )
    return jax.shard_map(
        per_device, mesh=mesh, in_specs=in_specs, out_specs=out_specs, check_vma=False
    )
```

```python
import functools
import math

import jax
import jax.numpy as jnp
import numpy as np
from jax import lax
from jax.experimental import pallas as pl
from jax.experimental.pallas import tpu as pltpu
from jax.sharding import PartitionSpec as P

GY = 8
STEPS = 4


STENCIL_COEF = (-205.0 / 72.0, 8.0 / 5.0, -1.0 / 5.0, 8.0 / 315.0, -1.0 / 560.0)


MESH = pl.DeviceIdType.MESH
HIGHEST = lax.Precision.HIGHEST


def dot_f32(left, right, left_dim=1, right_dim=0):
    return lax.dot_general(
        left,
        right,
        (((left_dim,), (right_dim,)), ((), ())),
        precision=HIGHEST,
        preferred_element_type=jnp.float32,
    )


def stencil_tables(z_depth, y_cols, chunk):
    coef = np.array(STENCIL_COEF, np.float64)
    halo = 4 * z_depth
    row = np.arange(chunk)[:, None]
    col = np.arange(chunk + 2 * halo)[None, :] - halo
    dx = np.abs(row // z_depth - col // z_depth)
    dz = np.abs(row % z_depth - col % z_depth)
    band = np.where((dz == 0) & (dx <= 4), coef[np.minimum(dx, 4)], 0.0)
    band = band + np.where((dx == 0) & (dz <= 4), coef[np.minimum(dz, 4)], 0.0)
    lane = np.arange(y_cols)
    dy = np.abs(lane[:, None] - lane[None, :])
    along_y = np.where(dy <= 4, coef[np.minimum(dy, 4)], 0.0)
    along_y = np.kron(np.eye(2), along_y)
    edge = np.arange(halo)
    near = edge[:, None] // z_depth + 4 - edge[None, :] // z_depth
    same = edge[:, None] % z_depth == edge[None, :] % z_depth
    from_low = np.where(same & (near <= 4), coef[np.minimum(near, 4)], 0.0)
    far = 4 + edge[None, :] // z_depth - edge[:, None] // z_depth
    from_high = np.where(same & (far <= 4), coef[np.minimum(far, 4)], 0.0)
    rim = np.zeros((16, 2 * y_cols))
    for field in range(2):
        for depth in range(4):
            for y in range(4):
                if y + 4 - depth <= 4:
                    rim[field * 4 + depth, field * y_cols + y] = coef[y + 4 - depth]
                last = y_cols - 1 - y
                gap = y_cols + depth - last
                if gap <= 4:
                    rim[8 + field * 4 + depth, field * y_cols + last] = coef[gap]
    pick = np.zeros((16, 2 * y_cols))
    for field in range(2):
        for depth in range(4):
            pick[field * 4 + depth, field * y_cols + depth] = 1.0
            pick[8 + field * 4 + depth, field * y_cols + y_cols - 4 + depth] = 1.0
    tables = (band, along_y, from_low, from_high, rim, pick)
    return [jnp.asarray(table.astype(np.float32)) for table in tables]


def plane_and_part(tile, planes):
    share = GY // planes
    column = lax.rem(tile, GY)
    return column // share, tile // GY * share + lax.rem(column, share)


def plane_holder(plane, part, planes):
    share = GY // planes
    return part // share * GY + plane * share + lax.rem(part, share)


def window_kernel(
    chunk, move_mass,
    model_ref, prev_ref, cur_ref, next_ref, now_ref, rec_ref, mass_ref,
    band_ref, along_ref, low_ref, high_ref, rim_ref, pick_ref,
    grad_ref, first_ref, second_ref, mass_out,
    both, lap, images, waves, adjoints, records, hot, weights, inject,
    x_out, x_in, y_out, y_in, halo_send, halo_recv, rec_send, rec_recv, own_sem,
    mass_in, mass_send, mass_recv, mass_own,
):
    chain = lax.axis_index("chain")
    tile = lax.axis_index("gx")
    devices = lax.axis_size("gx")
    x_blocks = devices // GY
    rows, y_cols = model_ref.shape
    halo = x_out.shape[2]
    column = lax.rem(tile, GY)
    block = tile // GY
    neighbours = (
        lax.rem(block + x_blocks - 1, x_blocks) * GY + column,
        lax.rem(block + 1, x_blocks) * GY + column,
        block * GY + lax.rem(column + GY - 1, GY),
        block * GY + lax.rem(column + 1, GY),
    )
    has_low = (block > 0).astype(jnp.float32)
    has_high = (block < x_blocks - 1).astype(jnp.float32)
    has_left = (column > 0).astype(jnp.float32)
    has_right = (column < GY - 1).astype(jnp.float32)

    own = pltpu.make_async_copy(rec_ref, records.at[0], own_sem)
    own.start()
    barrier = pltpu.get_barrier_semaphore()

    @pl.loop(1, devices)
    def _(step):
        pl.semaphore_signal(
            barrier, inc=1, device_id=(chain, lax.rem(tile + step, devices)), device_id_type=MESH
        )

    both[0:halo, :] = jnp.zeros((halo, 2 * y_cols), jnp.float32)
    both[halo + rows :, :] = jnp.zeros((halo, 2 * y_cols), jnp.float32)
    low_rows = lax.broadcasted_iota(jnp.int32, rim_ref.shape, 0) < 8
    rim = rim_ref[...] * jnp.where(low_rows, has_left, has_right)

    along = halves(along_ref[...])
    band = halves(band_ref[...])

    def pack(phase, wave, adjoint):
        both[halo : halo + rows, 0:y_cols] = wave
        both[halo : halo + rows, y_cols:] = model_ref[...] * adjoint
        x_out[phase, 0] = both[halo : 2 * halo, :]
        x_out[phase, 1] = both[rows : halo + rows, :]
        high, low = halves(both[...])
        picked = pick_ref[...].astype(jnp.bfloat16)
        strips = sum(
            lax.dot_general(
                picked,
                level[halo : halo + rows],
                (((1,), (1,)), ((), ())),
                preferred_element_type=jnp.float32,
            )
            for level in (high, low)
        )
        y_out[phase, 0] = strips[0:8]
        y_out[phase, 1] = strips[8:16]
        return high, low

    def halo_copies(phase):
        copies = []
        for way in range(4):
            source = x_out if way < 2 else y_out
            target = x_in if way < 2 else y_in
            copies.append(
                pltpu.make_async_remote_copy(
                    src_ref=source.at[phase, way % 2],
                    dst_ref=target.at[phase, 1 - way % 2],
                    send_sem=halo_send.at[phase, way],
                    recv_sem=halo_recv.at[phase, way],
                    device_id=(chain, neighbours[way]),
                    device_id_type=MESH,
                )
            )
        return copies

    def record_copy(step):
        return pltpu.make_async_remote_copy(
            src_ref=rec_ref,
            dst_ref=records.at[step],
            send_sem=rec_send.at[step],
            recv_sem=rec_recv.at[step],
            device_id=(chain, lax.rem(tile + step, devices)),
            device_id_type=MESH,
        )

    slots = mass_in.shape[0]
    _, quarter = plane_and_part(tile, slots)

    def mass_copies(number):
        target = plane_holder(number, tile // slots, slots)
        remote = pltpu.make_async_remote_copy(
            src_ref=mass_ref,
            dst_ref=mass_in.at[lax.rem(tile, slots)],
            send_sem=mass_send.at[number],
            recv_sem=mass_recv.at[lax.rem(tile, slots)],
            device_id=(chain, target),
            device_id_type=MESH,
        )
        local = pltpu.make_async_copy(mass_ref, mass_in.at[lax.rem(tile, slots)], mass_own)
        return target != tile, remote, local

    def mass_start():
        for number in range(slots):
            away, remote, local = mass_copies(number)
            pl.when(away)(remote.start)
            pl.when(jnp.logical_not(away))(local.start)

    def mass_finish():
        for number in range(slots):
            away, remote, local = mass_copies(number)
            pl.when(away)(remote.wait_send)
            pl.when(jnp.logical_not(away))(local.wait)
        for slot in range(slots):
            arrival = pltpu.make_async_remote_copy(
                src_ref=mass_ref,
                dst_ref=mass_in.at[slot],
                send_sem=mass_send.at[slot],
                recv_sem=mass_recv.at[slot],
                device_id=(chain, lax.rem(tile + 1, devices)),
                device_id_type=MESH,
            )
            pl.when(quarter * slots + slot != tile)(arrival.wait_recv)
        mass_out[...] = mass_in[...]

    high, low = pack(0, cur_ref[...], now_ref[...])
    pl.semaphore_wait(barrier, devices - 1)
    pending = []
    width = rec_ref.shape[1]
    total = devices * width
    part = math.gcd(total, 2048)
    for phase in range(STEPS):
        copies = halo_copies(phase)
        for copy in copies:
            copy.start()
        pending += copies
        if phase == 0:

            @pl.loop(1, devices)
            def _(step):
                record_copy(step).start()

            if move_mass:
                mass_start()

        for start in range(0, rows, chunk):
            inner = slice(halo + start, halo + start + chunk)
            outer = slice(start, start + chunk + 2 * halo)
            lap[start : start + chunk, :] = dot_halves(
                (high[inner], low[inner]), along
            ) + dot_halves(band, (high[outer], low[outer]))
        if phase == 0:
            own.wait()

            @pl.loop(1, devices)
            def _(step):
                record_copy(step).wait()

            @pl.loop(0, devices)
            def _(step):
                lanes = pl.ds(pl.multiple_of(step * width, width), width)
                cell = records[step, 0:1, :] - (tile * rows).astype(jnp.float32)
                index = lax.broadcasted_iota(jnp.int32, (rows, width), 0).astype(jnp.float32)
                hot[:, lanes] = jnp.where(index == cell, 1.0, 0.0).astype(jnp.bfloat16)

        section = STEPS - 1 - phase

        @pl.loop(0, devices)
        def _(step):
            lanes = pl.ds(pl.multiple_of(step * width, width), width)
            place = records[step, 1:2, :]
            value = records[step, 2 + section : 3 + section, :]
            index = lax.broadcasted_iota(jnp.int32, (y_cols, width), 0).astype(jnp.float32)
            rest = jnp.where(index == place, value, 0.0)
            for level in range(2):
                piece = rest.astype(jnp.bfloat16)
                weights[level * y_cols : (level + 1) * y_cols, lanes] = piece
                rest = rest - piece.astype(jnp.float32)

        def injected(lanes):
            pair = lax.dot_general(
                hot[:, lanes],
                weights[:, lanes],
                (((1,), (1,)), ((), ())),
                preferred_element_type=jnp.float32,
            )
            return pair[:, 0:y_cols] + pair[:, y_cols:]

        inject[...] = injected(pl.ds(0, part))
        if total > part:

            @pl.loop(1, total // part)
            def _(step):
                inject[...] += injected(pl.ds(pl.multiple_of(step * part, part), part))

        for copy in copies:
            copy.wait_recv()
        sides = jnp.concatenate((y_in[phase, 0], y_in[phase, 1]), axis=0)
        lap[...] += dot_f32(sides, rim, 0, 0)
        lap[0:halo, :] += has_low * dot_f32(low_ref[...], x_in[phase, 0])
        lap[rows - halo :, :] += has_high * dot_f32(high_ref[...], x_in[phase, 1])
        image = lap[:, 0:y_cols]
        images[phase] = image
        if phase + 1 < STEPS:
            older = prev_ref[...] if phase == 0 else (cur_ref[...] if phase == 1 else waves[0])
            newer = cur_ref[...] if phase == 0 else waves[phase - 1]
            waves[phase] = 2.0 * newer - older + model_ref[...] * image
        later = next_ref[...] if phase == 0 else (now_ref[...] if phase == 1 else adjoints[phase - 2])
        now = now_ref[...] if phase == 0 else adjoints[phase - 1]
        adjoints[phase] = 2.0 * now - later + lap[:, y_cols:] + inject[...]
        if phase + 1 < STEPS:
            high, low = pack(phase + 1, waves[phase], adjoints[phase])
    grad_ref[...] = (
        now_ref[...] * images[3]
        + adjoints[0] * images[2]
        + adjoints[1] * images[1]
        + adjoints[2] * images[0]
    )
    first_ref[...] = adjoints[3]
    second_ref[...] = adjoints[2]
    for copy in pending:
        copy.wait_send()
    if move_mass:
        mass_finish()
    else:
        mass_out[...] = jnp.zeros(mass_out.shape, jnp.float32)


def run_window(model, u_prev, u_cur, a_next, a_cur, records, mass, move_mass):
    rows, y_cols = model.shape
    z_depth = 4
    devices = lax.axis_size("gx")
    halo = 4 * z_depth
    chunk = 128
    total = devices * records.shape[1]
    tables = stencil_tables(z_depth, y_cols, chunk)
    field = jax.ShapeDtypeStruct((rows, y_cols), jnp.float32)
    slots = jax.ShapeDtypeStruct((z_depth,) + mass.shape, jnp.float32)
    vmem = pl.BlockSpec(memory_space=pltpu.VMEM)
    return pl.pallas_call(
        functools.partial(window_kernel, chunk, move_mass),
        out_shape=(field, field, field, slots),
        in_specs=[vmem] * 13,
        out_specs=(vmem,) * 4,
        scratch_shapes=[
            pltpu.VMEM((rows + 2 * halo, 2 * y_cols), jnp.float32),
            pltpu.VMEM((rows, 2 * y_cols), jnp.float32),
            pltpu.VMEM((STEPS, rows, y_cols), jnp.float32),
            pltpu.VMEM((STEPS - 1, rows, y_cols), jnp.float32),
            pltpu.VMEM((STEPS, rows, y_cols), jnp.float32),
            pltpu.VMEM((devices,) + records.shape, jnp.float32),
            pltpu.VMEM((rows, total), jnp.bfloat16),
            pltpu.VMEM((2 * y_cols, total), jnp.bfloat16),
            pltpu.VMEM((rows, y_cols), jnp.float32),
            pltpu.VMEM((STEPS, 2, halo, 2 * y_cols), jnp.float32),
            pltpu.VMEM((STEPS, 2, halo, 2 * y_cols), jnp.float32),
            pltpu.VMEM((STEPS, 2, 8, rows), jnp.float32),
            pltpu.VMEM((STEPS, 2, 8, rows), jnp.float32),
            pltpu.SemaphoreType.DMA((STEPS, 4)),
            pltpu.SemaphoreType.DMA((STEPS, 4)),
            pltpu.SemaphoreType.DMA((devices,)),
            pltpu.SemaphoreType.DMA((devices,)),
            pltpu.SemaphoreType.DMA,
            pltpu.VMEM(slots.shape, jnp.float32),
            pltpu.SemaphoreType.DMA((z_depth,)),
            pltpu.SemaphoreType.DMA((z_depth,)),
            pltpu.SemaphoreType.DMA,
        ],
        compiler_params=pltpu.CompilerParams(
            collective_id=0, has_side_effects=True, vmem_limit_bytes=56 * 2**20
        ),
    )(model, u_prev, u_cur, a_next, a_cur, records, mass, *tables)


def halves(value):
    high = value.astype(jnp.bfloat16)
    return high, (value - high.astype(jnp.float32)).astype(jnp.bfloat16)


def dot_halves(left, right, right_dim=0):
    def product(a, b):
        return lax.dot_general(
            a, b, (((1,), (right_dim,)), ((), ())), preferred_element_type=jnp.float32
        )

    return product(left[0], right[0]) + (product(left[0], right[1]) + product(left[1], right[0]))


def spectral_kernel(
    grad_ref, mass_ref, x_high_ref, x_low_ref, y_ref,
    out_ref,
    arrived, spectrum, y_table, y_high, y_low, back_high, back_low, leaving, partial,
    send_one, recv_one, send_two, recv_two, table_sem,
):
    chain = lax.axis_index("chain")
    tile = lax.axis_index("gx")
    devices = lax.axis_size("gx")
    planes, x_rows, y_cols = grad_ref.shape
    x_total = spectrum.shape[0]
    width = spectrum.shape[1] // 2
    plane, part = plane_and_part(tile, planes)

    load = pltpu.make_async_copy(y_ref.at[part], y_table, table_sem)
    load.start()
    barrier = pltpu.get_barrier_semaphore()

    @pl.loop(1, devices)
    def _(step):
        pl.semaphore_signal(
            barrier, inc=1, device_id=(chain, lax.rem(tile + step, devices)), device_id_type=MESH
        )

    sibling = tile + 1 - 2 * lax.rem(tile, 2)
    turns = devices // 2

    def copy_to(peer, source, target, send_sem, recv_sem):
        return pltpu.make_async_remote_copy(
            src_ref=source,
            dst_ref=target,
            send_sem=send_sem,
            recv_sem=recv_sem,
            device_id=(chain, peer),
            device_id_type=MESH,
        )

    def ahead(first, turn):
        return lax.rem(first + 2 * turn, devices)

    def behind(first, turn):
        return lax.rem(first + devices - 2 * turn, devices)

    def outward(turn):
        peer = ahead(tile, turn)
        slot = 2 * turn
        source = grad_ref.at[plane_and_part(peer, planes)[0]]
        return copy_to(peer, source, arrived.at[slot], send_one.at[slot], recv_one.at[slot])

    def forward(turn):
        slot = 2 * turn + 1
        return copy_to(
            sibling, arrived.at[2 * turn], arrived.at[slot], send_one.at[slot], recv_one.at[slot]
        )

    def homeward(turn):
        slot = 2 * turn
        return copy_to(
            ahead(tile, turn), leaving.at[slot], partial.at[slot], send_two.at[slot], recv_two.at[slot]
        )

    def across(turn):
        slot = 2 * turn + 1
        return copy_to(
            sibling, leaving.at[slot], partial.at[slot], send_two.at[slot], recv_two.at[slot]
        )

    spectrum[...] = jnp.zeros(spectrum.shape, jnp.float32)
    pl.semaphore_wait(barrier, devices - 1)

    @pl.loop(1, turns)
    def _(turn):
        outward(turn).start()

    arrived[0] = grad_ref[plane]
    forward(0).start()
    load.wait()
    y_high[...], y_low[...] = halves(y_table[...])

    def block_rows(owner):
        return pl.ds(pl.multiple_of(owner // GY * x_rows, x_rows), x_rows)

    def table_rows(owner):
        return pl.ds(pl.multiple_of(lax.rem(owner, GY) * y_cols, y_cols), y_cols)

    def transform(owner, value):
        lines = table_rows(owner)
        spectrum[block_rows(owner), :] += dot_halves(
            halves(value), (y_high[lines, :], y_low[lines, :])
        )

    transform(tile, grad_ref[plane])

    def take_forwarded(turn):
        forward(turn).wait_recv()
        transform(behind(sibling, turn), arrived[2 * turn + 1])

    @pl.loop(1, turns)
    def _(turn):
        outward(turn).wait_recv()
        forward(turn).start()
        transform(behind(tile, turn), arrived[2 * turn])
        take_forwarded(turn - 1)

    take_forwarded(turns - 1)

    def along_x(value, orient):
        mixed = dot_halves((x_high_ref[...], x_low_ref[...]), halves(value))
        cosine, sine = mixed[0:x_total], mixed[x_total:]
        real = cosine[:, 0:width] - orient * sine[:, width:]
        imag = cosine[:, width:] + orient * sine[:, 0:width]
        return real, imag

    real, imag = along_x(spectrum[...], -1.0)
    spectrum[:, 0:width] = real * mass_ref[...]
    spectrum[:, width:] = imag * mass_ref[...]
    real, imag = along_x(spectrum[...], 1.0)
    back_high[:, 0:width], back_low[:, 0:width] = halves(real)
    back_high[:, width:], back_low[:, width:] = halves(imag)

    def restored(owner):
        rows, lines = block_rows(owner), table_rows(owner)
        return dot_halves(
            (back_high[rows, :], back_low[rows, :]), (y_high[lines, :], y_low[lines, :]), 1
        )

    def pass_across(turn):
        leaving[2 * turn + 1] = restored(ahead(sibling, turn))
        across(turn).start()

    pass_across(1)

    @pl.loop(1, turns)
    def _(turn):
        pass_across(lax.rem(turn + 1, turns))
        own = restored(ahead(tile, turn))
        across(turn).wait_recv()
        leaving[2 * turn] = own + partial[2 * turn + 1]
        homeward(turn).start()

    out_ref[...] = jnp.zeros(out_ref.shape, jnp.float32)
    mine = restored(tile)
    across(0).wait_recv()
    out_ref[plane] += mine + partial[1]

    @pl.loop(1, turns)
    def _(turn):
        homeward(turn).wait_recv()
        out_ref[plane_and_part(behind(tile, turn), planes)[0]] += partial[2 * turn]

    forward(0).wait_send()
    across(0).wait_send()

    @pl.loop(1, turns)
    def _(turn):
        outward(turn).wait_send()
        forward(turn).wait_send()
        across(turn).wait_send()
        homeward(turn).wait_send()


def table_halves(table):
    high = table.astype(jnp.bfloat16)
    low = (table - high.astype(np.float64)).astype(jnp.bfloat16)
    return jnp.asarray(high), jnp.asarray(low)


def run_spectral(grad, mass):
    planes, x_rows, y_cols = grad.shape
    devices = lax.axis_size("gx")
    x_total, width = mass.shape
    y_total = y_cols * GY
    parts = y_total // width
    turn = np.arange(x_total)[:, None] * np.arange(x_total)[None, :] % x_total
    angle = turn * (2.0 * np.pi / x_total)
    x_tables = table_halves(np.concatenate((np.cos(angle), np.sin(angle)), axis=0))
    turn = np.arange(y_total)[:, None] * np.arange(y_total)[None, :] % y_total
    angle = (turn * (2.0 * np.pi / y_total)).reshape(y_total, parts, width).transpose(1, 0, 2)
    y_table = np.concatenate((np.cos(angle), -np.sin(angle)), axis=2).astype(np.float32)
    vmem = pl.BlockSpec(memory_space=pltpu.VMEM)
    hbm = pl.BlockSpec(memory_space=pl.ANY)
    tiles = (devices, x_rows, y_cols)
    return pl.pallas_call(
        spectral_kernel,
        out_shape=jax.ShapeDtypeStruct(grad.shape, jnp.float32),
        in_specs=[vmem] * 4 + [hbm],
        out_specs=vmem,
        scratch_shapes=[
            pltpu.VMEM(tiles, jnp.float32),
            pltpu.VMEM((x_total, 2 * width), jnp.float32),
            pltpu.VMEM((y_total, 2 * width), jnp.float32),
            pltpu.VMEM((y_total, 2 * width), jnp.bfloat16),
            pltpu.VMEM((y_total, 2 * width), jnp.bfloat16),
            pltpu.VMEM((x_total, 2 * width), jnp.bfloat16),
            pltpu.VMEM((x_total, 2 * width), jnp.bfloat16),
            pltpu.VMEM(tiles, jnp.float32),
            pltpu.VMEM(tiles, jnp.float32),
            pltpu.SemaphoreType.DMA((devices,)),
            pltpu.SemaphoreType.DMA((devices,)),
            pltpu.SemaphoreType.DMA((devices,)),
            pltpu.SemaphoreType.DMA((devices,)),
            pltpu.SemaphoreType.DMA,
        ],
        compiler_params=pltpu.CompilerParams(
            collective_id=1, has_side_effects=True, vmem_limit_bytes=60 * 2**20
        ),
    )(grad, mass, *x_tables, jnp.asarray(y_table))


def pick_factor(length):
    candidate = math.isqrt(length)
    if candidate * candidate < length:
        candidate = candidate + 1
    while length % candidate != 0:
        candidate = candidate + 1
    return candidate


def phase_tables(rows_count, cols_count, modulus):
    first = jnp.arange(rows_count, dtype=jnp.int32)
    second = jnp.arange(cols_count, dtype=jnp.int32)
    phase_int = first[:, None] * second[None, :] % modulus
    angle_rad = phase_int.astype(jnp.float32) * (2.0 * math.pi / modulus)
    return (jnp.cos(angle_rad), jnp.sin(angle_rad))


def complex_mix(form, tab_cos, tab_sin, real_part, imag_part, orient):

    def product(table, data):
        return jnp.einsum(
            form, table, data, precision=lax.Precision.HIGHEST, preferred_element_type=jnp.float32
        )

    out_real = product(tab_cos, real_part) - orient * product(tab_sin, imag_part)
    out_imag = product(tab_cos, imag_part) + orient * product(tab_sin, real_part)
    return (out_real, out_imag)


def transform_rows(real_part, imag_part, orient):
    length, width = real_part.shape
    outer_len = pick_factor(length)
    inner_len = length // outer_len
    data_re = real_part.reshape(outer_len, inner_len, width)
    data_im = imag_part.reshape(outer_len, inner_len, width)
    cos_outer, sin_outer = phase_tables(outer_len, outer_len, outer_len)
    mid_re, mid_im = complex_mix("ca,abm->cbm", cos_outer, sin_outer, data_re, data_im, orient)
    twist_cos, twist_sin = phase_tables(outer_len, inner_len, length)
    twist_cos = twist_cos[:, :, None]
    twist_sin = twist_sin[:, :, None]
    turned_re = mid_re * twist_cos - orient * mid_im * twist_sin
    turned_im = mid_im * twist_cos + orient * mid_re * twist_sin
    cos_inner, sin_inner = phase_tables(inner_len, inner_len, inner_len)
    final_re, final_im = complex_mix(
        "db,cbm->dcm", cos_inner, sin_inner, turned_re, turned_im, orient
    )
    return (final_re.reshape(length, width), final_im.reshape(length, width))


def per_device(
    courant, ckpt_prev, ckpt_cur, adj_next, adj_cur, rec_x, rec_plane, traces, mass_kernel
):
    x_rows, z_depth, y_cols = courant.shape[1:]
    devices = lax.axis_size("gx")
    x_blocks = devices // GY
    x_total = x_rows * x_blocks
    y_total = y_cols * GY
    cell_y = rec_plane % y_total
    cell_z = rec_plane // y_total
    owner = rec_x // x_rows * GY + cell_y // y_cols
    cell_row = (owner * x_rows + rec_x % x_rows) * z_depth + cell_z
    records = jnp.concatenate(
        (
            cell_row.astype(jnp.float32)[None],
            (cell_y % y_cols).astype(jnp.float32)[None],
            traces,
            jnp.zeros((6 - STEPS, rec_x.shape[0]), jnp.float32),
        ),
        axis=0,
    )
    dense = x_total <= 512 and GY == 2 * z_depth and devices % z_depth == 0
    mass = mass_kernel.reshape(-1, 128) if dense else jnp.zeros((8, 128), jnp.float32)
    gradient, adj_now, adj_later, mass_slots = run_window(
        *(
            field.reshape(x_rows * z_depth, y_cols)
            for field in (courant, ckpt_prev, ckpt_cur, adj_next, adj_cur)
        ),
        records,
        mass,
        dense,
    )
    tile_shape = (1, x_rows, z_depth, y_cols)
    if dense:
        by_plane = gradient.reshape(x_rows, z_depth, y_cols).transpose(1, 0, 2)
        part_mass = mass_slots.reshape(z_depth, x_total, -1).transpose(1, 0, 2)
        part_mass = part_mass.reshape(x_total, -1) * (1.0 / (x_total * y_total))
        scaled = run_spectral(by_plane, part_mass).transpose(1, 0, 2)
        return (
            scaled.reshape(tile_shape),
            adj_now.reshape(tile_shape),
            adj_later.reshape(tile_shape),
        )
    flat_grad = gradient.reshape(x_rows * z_depth, 1, y_cols)
    rows = lax.all_to_all(flat_grad, "gx", split_axis=0, concat_axis=1, tiled=True)
    share = rows.shape[0]
    lines = rows.reshape(share * x_blocks, y_total).T
    spec_re_t, spec_im_t = transform_rows(lines, jnp.zeros_like(lines), -1.0)
    spec_re = spec_re_t.T.reshape(share, x_blocks, y_total)
    spec_im = spec_im_t.T.reshape(share, x_blocks, y_total)
    cols_re, cols_im = (
        lax.all_to_all(spec_re, "gx", split_axis=2, concat_axis=0, tiled=True),
        lax.all_to_all(spec_im, "gx", split_axis=2, concat_axis=0, tiled=True),
    )
    col_width = cols_re.shape[2]
    half_width = z_depth * col_width

    def to_columns(part):
        return (
            part.reshape(x_rows, z_depth, x_blocks, col_width)
            .transpose(2, 0, 1, 3)
            .reshape(x_total, half_width)
        )

    def from_columns(part):
        return (
            part.reshape(x_blocks, x_rows, z_depth, col_width)
            .transpose(1, 2, 0, 3)
            .reshape(devices * share, x_blocks, col_width)
        )

    freq_re, freq_im = transform_rows(to_columns(cols_re), to_columns(cols_im), -1.0)
    kernel_scale = (
        jnp.broadcast_to(mass_kernel[:, None, :], (x_total, z_depth, col_width)).reshape(
            x_total, half_width
        )
        / x_total
    )
    freq_re = freq_re * kernel_scale
    freq_im = freq_im * kernel_scale
    spat_re, spat_im = transform_rows(freq_re, freq_im, 1.0)
    back_re = from_columns(spat_re)
    back_im = from_columns(spat_im)
    line_re, line_im = (
        lax.all_to_all(back_re, "gx", split_axis=0, concat_axis=2, tiled=True),
        lax.all_to_all(back_im, "gx", split_axis=0, concat_axis=2, tiled=True),
    )
    lines_re = line_re.reshape(share * x_blocks, y_total).T
    lines_im = line_im.reshape(share * x_blocks, y_total).T
    real_t, imag_t = transform_rows(lines_re, lines_im, 1.0)
    real_lines = (real_t.T / y_total).reshape(share, devices, y_cols)
    tiled = lax.all_to_all(real_lines, "gx", split_axis=1, concat_axis=0, tiled=True)
    return (tiled.reshape(tile_shape), adj_now.reshape(tile_shape), adj_later.reshape(tile_shape))


def solution(mesh):
    in_specs = (
        P(("chain", "gx"), None, None, None),
        P(("chain", "gx"), None, None, None),
        P(("chain", "gx"), None, None, None),
        P(("chain", "gx"), None, None, None),
        P(("chain", "gx"), None, None, None),
        P(("chain", "gx")),
        P(("chain", "gx")),
        P(None, ("chain", "gx")),
        P(None, "gx"),
    )
    out_specs = (
        P(("chain", "gx"), None, None, None),
        P(("chain", "gx"), None, None, None),
        P(("chain", "gx"), None, None, None),
    )
    return jax.shard_map(
        per_device, mesh=mesh, in_specs=in_specs, out_specs=out_specs, check_vma=False
    )
```

```python
import functools
import math

import jax
import jax.numpy as jnp
import numpy as np
from jax import lax
from jax.experimental import pallas as pl
from jax.experimental.pallas import tpu as pltpu
from jax.sharding import PartitionSpec as P

GY = 8
STEPS = 4


STENCIL_COEF = (-205.0 / 72.0, 8.0 / 5.0, -1.0 / 5.0, 8.0 / 315.0, -1.0 / 560.0)


MESH = pl.DeviceIdType.MESH
HIGHEST = lax.Precision.HIGHEST


def dot_f32(left, right, left_dim=1, right_dim=0):
    return lax.dot_general(
        left,
        right,
        (((left_dim,), (right_dim,)), ((), ())),
        precision=HIGHEST,
        preferred_element_type=jnp.float32,
    )


def stencil_tables(z_depth, y_cols, chunk):
    coef = np.array(STENCIL_COEF, np.float64)
    halo = 4 * z_depth
    row = np.arange(chunk)[:, None]
    col = np.arange(chunk + 2 * halo)[None, :] - halo
    dx = np.abs(row // z_depth - col // z_depth)
    dz = np.abs(row % z_depth - col % z_depth)
    band = np.where((dz == 0) & (dx <= 4), coef[np.minimum(dx, 4)], 0.0)
    band = band + np.where((dx == 0) & (dz <= 4), coef[np.minimum(dz, 4)], 0.0)
    lane = np.arange(y_cols)
    dy = np.abs(lane[:, None] - lane[None, :])
    along_y = np.where(dy <= 4, coef[np.minimum(dy, 4)], 0.0)
    along_y = np.kron(np.eye(2), along_y)
    edge = np.arange(halo)
    near = edge[:, None] // z_depth + 4 - edge[None, :] // z_depth
    same = edge[:, None] % z_depth == edge[None, :] % z_depth
    from_low = np.where(same & (near <= 4), coef[np.minimum(near, 4)], 0.0)
    far = 4 + edge[None, :] // z_depth - edge[:, None] // z_depth
    from_high = np.where(same & (far <= 4), coef[np.minimum(far, 4)], 0.0)
    rim = np.zeros((16, 2 * y_cols))
    for field in range(2):
        for depth in range(4):
            for y in range(4):
                if y + 4 - depth <= 4:
                    rim[field * 4 + depth, field * y_cols + y] = coef[y + 4 - depth]
                last = y_cols - 1 - y
                gap = y_cols + depth - last
                if gap <= 4:
                    rim[8 + field * 4 + depth, field * y_cols + last] = coef[gap]
    pick = np.zeros((16, 2 * y_cols))
    for field in range(2):
        for depth in range(4):
            pick[field * 4 + depth, field * y_cols + depth] = 1.0
            pick[8 + field * 4 + depth, field * y_cols + y_cols - 4 + depth] = 1.0
    tables = (band, along_y, from_low, from_high, rim, pick)
    return [jnp.asarray(table.astype(np.float32)) for table in tables]


def plane_and_part(tile, planes):
    share = GY // planes
    column = lax.rem(tile, GY)
    return column // share, tile // GY * share + lax.rem(column, share)


def plane_holder(plane, part, planes):
    share = GY // planes
    return part // share * GY + plane * share + lax.rem(part, share)


def window_kernel(
    chunk, move_mass,
    model_ref, prev_ref, cur_ref, next_ref, now_ref, rec_ref, mass_ref,
    band_ref, along_ref, low_ref, high_ref, rim_ref, pick_ref,
    grad_ref, first_ref, second_ref, mass_out,
    both, lap, images, waves, adjoints, records, hot, weights, inject,
    x_out, x_in, y_out, y_in, halo_send, halo_recv, rec_send, rec_recv, own_sem,
    mass_in, mass_send, mass_recv, mass_own,
):
    chain = lax.axis_index("chain")
    tile = lax.axis_index("gx")
    devices = lax.axis_size("gx")
    x_blocks = devices // GY
    rows, y_cols = model_ref.shape
    halo = x_out.shape[2]
    column = lax.rem(tile, GY)
    block = tile // GY
    neighbours = (
        lax.rem(block + x_blocks - 1, x_blocks) * GY + column,
        lax.rem(block + 1, x_blocks) * GY + column,
        block * GY + lax.rem(column + GY - 1, GY),
        block * GY + lax.rem(column + 1, GY),
    )
    has_low = (block > 0).astype(jnp.float32)
    has_high = (block < x_blocks - 1).astype(jnp.float32)
    has_left = (column > 0).astype(jnp.float32)
    has_right = (column < GY - 1).astype(jnp.float32)

    own = pltpu.make_async_copy(rec_ref, records.at[0], own_sem)
    own.start()
    barrier = pltpu.get_barrier_semaphore()

    @pl.loop(1, devices)
    def _(step):
        pl.semaphore_signal(
            barrier, inc=1, device_id=(chain, lax.rem(tile + step, devices)), device_id_type=MESH
        )

    both[0:halo, :] = jnp.zeros((halo, 2 * y_cols), jnp.float32)
    both[halo + rows :, :] = jnp.zeros((halo, 2 * y_cols), jnp.float32)
    low_rows = lax.broadcasted_iota(jnp.int32, rim_ref.shape, 0) < 8
    rim = rim_ref[...] * jnp.where(low_rows, has_left, has_right)

    along = halves(along_ref[...])
    band = halves(band_ref[...])

    def pack(phase, wave, adjoint):
        both[halo : halo + rows, 0:y_cols] = wave
        both[halo : halo + rows, y_cols:] = model_ref[...] * adjoint
        x_out[phase, 0] = both[halo : 2 * halo, :]
        x_out[phase, 1] = both[rows : halo + rows, :]
        high, low = halves(both[...])
        picked = pick_ref[...].astype(jnp.bfloat16)
        strips = sum(
            lax.dot_general(
                picked,
                level[halo : halo + rows],
                (((1,), (1,)), ((), ())),
                preferred_element_type=jnp.float32,
            )
            for level in (high, low)
        )
        y_out[phase, 0] = strips[0:8]
        y_out[phase, 1] = strips[8:16]
        return high, low

    def halo_copies(phase):
        copies = []
        for way in range(4):
            source = x_out if way < 2 else y_out
            target = x_in if way < 2 else y_in
            copies.append(
                pltpu.make_async_remote_copy(
                    src_ref=source.at[phase, way % 2],
                    dst_ref=target.at[phase, 1 - way % 2],
                    send_sem=halo_send.at[phase, way],
                    recv_sem=halo_recv.at[phase, way],
                    device_id=(chain, neighbours[way]),
                    device_id_type=MESH,
                )
            )
        return copies

    def record_copy(step):
        return pltpu.make_async_remote_copy(
            src_ref=rec_ref,
            dst_ref=records.at[step],
            send_sem=rec_send.at[step],
            recv_sem=rec_recv.at[step],
            device_id=(chain, lax.rem(tile + step, devices)),
            device_id_type=MESH,
        )

    slots = mass_in.shape[0]
    _, quarter = plane_and_part(tile, slots)

    def mass_copies(number):
        target = plane_holder(number, tile // slots, slots)
        remote = pltpu.make_async_remote_copy(
            src_ref=mass_ref,
            dst_ref=mass_in.at[lax.rem(tile, slots)],
            send_sem=mass_send.at[number],
            recv_sem=mass_recv.at[lax.rem(tile, slots)],
            device_id=(chain, target),
            device_id_type=MESH,
        )
        local = pltpu.make_async_copy(mass_ref, mass_in.at[lax.rem(tile, slots)], mass_own)
        return target != tile, remote, local

    def mass_start():
        for number in range(slots):
            away, remote, local = mass_copies(number)
            pl.when(away)(remote.start)
            pl.when(jnp.logical_not(away))(local.start)

    def mass_finish():
        for number in range(slots):
            away, remote, local = mass_copies(number)
            pl.when(away)(remote.wait_send)
            pl.when(jnp.logical_not(away))(local.wait)
        for slot in range(slots):
            arrival = pltpu.make_async_remote_copy(
                src_ref=mass_ref,
                dst_ref=mass_in.at[slot],
                send_sem=mass_send.at[slot],
                recv_sem=mass_recv.at[slot],
                device_id=(chain, lax.rem(tile + 1, devices)),
                device_id_type=MESH,
            )
            pl.when(quarter * slots + slot != tile)(arrival.wait_recv)
        mass_out[...] = mass_in[...]

    high, low = pack(0, cur_ref[...], now_ref[...])
    pl.semaphore_wait(barrier, devices - 1)
    pending = []
    width = rec_ref.shape[1]
    total = devices * width
    part = math.gcd(total, 2048)
    for phase in range(STEPS):
        copies = halo_copies(phase)
        for copy in copies:
            copy.start()
        pending += copies
        if phase == 0:

            @pl.loop(1, devices)
            def _(step):
                record_copy(step).start()

            if move_mass:
                mass_start()

        for start in range(0, rows, chunk):
            inner = slice(halo + start, halo + start + chunk)
            outer = slice(start, start + chunk + 2 * halo)
            lap[start : start + chunk, :] = dot_halves(
                (high[inner], low[inner]), along
            ) + dot_halves(band, (high[outer], low[outer]))
        if phase == 0:
            own.wait()

            @pl.loop(1, devices)
            def _(step):
                record_copy(step).wait()

            @pl.loop(0, devices)
            def _(step):
                lanes = pl.ds(pl.multiple_of(step * width, width), width)
                cell = records[step, 0:1, :] - (tile * rows).astype(jnp.float32)
                index = lax.broadcasted_iota(jnp.int32, (rows, width), 0).astype(jnp.float32)
                hot[:, lanes] = jnp.where(index == cell, 1.0, 0.0).astype(jnp.bfloat16)

        section = STEPS - 1 - phase

        @pl.loop(0, devices)
        def _(step):
            lanes = pl.ds(pl.multiple_of(step * width, width), width)
            place = records[step, 1:2, :]
            value = records[step, 2 + section : 3 + section, :]
            index = lax.broadcasted_iota(jnp.int32, (y_cols, width), 0).astype(jnp.float32)
            rest = jnp.where(index == place, value, 0.0)
            for level in range(2):
                piece = rest.astype(jnp.bfloat16)
                weights[level * y_cols : (level + 1) * y_cols, lanes] = piece
                rest = rest - piece.astype(jnp.float32)

        def injected(lanes):
            pair = lax.dot_general(
                hot[:, lanes],
                weights[:, lanes],
                (((1,), (1,)), ((), ())),
                preferred_element_type=jnp.float32,
            )
            return pair[:, 0:y_cols] + pair[:, y_cols:]

        inject[...] = injected(pl.ds(0, part))
        if total > part:

            @pl.loop(1, total // part)
            def _(step):
                inject[...] += injected(pl.ds(pl.multiple_of(step * part, part), part))

        for copy in copies:
            copy.wait_recv()
        sides = jnp.concatenate((y_in[phase, 0], y_in[phase, 1]), axis=0)
        lap[...] += dot_f32(sides, rim, 0, 0)
        lap[0:halo, :] += has_low * dot_f32(low_ref[...], x_in[phase, 0])
        lap[rows - halo :, :] += has_high * dot_f32(high_ref[...], x_in[phase, 1])
        image = lap[:, 0:y_cols]
        images[phase] = image
        if phase + 1 < STEPS:
            older = prev_ref[...] if phase == 0 else (cur_ref[...] if phase == 1 else waves[0])
            newer = cur_ref[...] if phase == 0 else waves[phase - 1]
            waves[phase] = 2.0 * newer - older + model_ref[...] * image
        later = next_ref[...] if phase == 0 else (now_ref[...] if phase == 1 else adjoints[phase - 2])
        now = now_ref[...] if phase == 0 else adjoints[phase - 1]
        adjoints[phase] = 2.0 * now - later + lap[:, y_cols:] + inject[...]
        if phase + 1 < STEPS:
            high, low = pack(phase + 1, waves[phase], adjoints[phase])
    grad_ref[...] = (
        now_ref[...] * images[3]
        + adjoints[0] * images[2]
        + adjoints[1] * images[1]
        + adjoints[2] * images[0]
    )
    first_ref[...] = adjoints[3]
    second_ref[...] = adjoints[2]
    for copy in pending:
        copy.wait_send()
    if move_mass:
        mass_finish()
    else:
        mass_out[...] = jnp.zeros(mass_out.shape, jnp.float32)


def run_window(model, u_prev, u_cur, a_next, a_cur, records, mass, move_mass):
    rows, y_cols = model.shape
    z_depth = 4
    devices = lax.axis_size("gx")
    halo = 4 * z_depth
    chunk = 128
    total = devices * records.shape[1]
    tables = stencil_tables(z_depth, y_cols, chunk)
    field = jax.ShapeDtypeStruct((rows, y_cols), jnp.float32)
    slots = jax.ShapeDtypeStruct((z_depth,) + mass.shape, jnp.float32)
    vmem = pl.BlockSpec(memory_space=pltpu.VMEM)
    return pl.pallas_call(
        functools.partial(window_kernel, chunk, move_mass),
        out_shape=(field, field, field, slots),
        in_specs=[vmem] * 13,
        out_specs=(vmem,) * 4,
        scratch_shapes=[
            pltpu.VMEM((rows + 2 * halo, 2 * y_cols), jnp.float32),
            pltpu.VMEM((rows, 2 * y_cols), jnp.float32),
            pltpu.VMEM((STEPS, rows, y_cols), jnp.float32),
            pltpu.VMEM((STEPS - 1, rows, y_cols), jnp.float32),
            pltpu.VMEM((STEPS, rows, y_cols), jnp.float32),
            pltpu.VMEM((devices,) + records.shape, jnp.float32),
            pltpu.VMEM((rows, total), jnp.bfloat16),
            pltpu.VMEM((2 * y_cols, total), jnp.bfloat16),
            pltpu.VMEM((rows, y_cols), jnp.float32),
            pltpu.VMEM((STEPS, 2, halo, 2 * y_cols), jnp.float32),
            pltpu.VMEM((STEPS, 2, halo, 2 * y_cols), jnp.float32),
            pltpu.VMEM((STEPS, 2, 8, rows), jnp.float32),
            pltpu.VMEM((STEPS, 2, 8, rows), jnp.float32),
            pltpu.SemaphoreType.DMA((STEPS, 4)),
            pltpu.SemaphoreType.DMA((STEPS, 4)),
            pltpu.SemaphoreType.DMA((devices,)),
            pltpu.SemaphoreType.DMA((devices,)),
            pltpu.SemaphoreType.DMA,
            pltpu.VMEM(slots.shape, jnp.float32),
            pltpu.SemaphoreType.DMA((z_depth,)),
            pltpu.SemaphoreType.DMA((z_depth,)),
            pltpu.SemaphoreType.DMA,
        ],
        compiler_params=pltpu.CompilerParams(
            collective_id=0, has_side_effects=True, vmem_limit_bytes=56 * 2**20
        ),
    )(model, u_prev, u_cur, a_next, a_cur, records, mass, *tables)


def halves(value):
    high = value.astype(jnp.bfloat16)
    return high, (value - high.astype(jnp.float32)).astype(jnp.bfloat16)


def dot_halves(left, right, right_dim=0):
    def product(a, b):
        return lax.dot_general(
            a, b, (((1,), (right_dim,)), ((), ())), preferred_element_type=jnp.float32
        )

    return product(left[0], right[0]) + (product(left[0], right[1]) + product(left[1], right[0]))


def spectral_kernel(
    grad_ref, mass_ref, x_high_ref, x_low_ref, y_ref,
    out_ref,
    arrived, spectrum, y_table, y_high, y_low, back_high, back_low, leaving, partial,
    send_one, recv_one, send_two, recv_two, table_sem,
):
    chain = lax.axis_index("chain")
    tile = lax.axis_index("gx")
    devices = lax.axis_size("gx")
    planes, x_rows, y_cols = grad_ref.shape
    x_total = spectrum.shape[0]
    width = spectrum.shape[1] // 2
    plane, part = plane_and_part(tile, planes)

    load = pltpu.make_async_copy(y_ref.at[part], y_table, table_sem)
    load.start()
    barrier = pltpu.get_barrier_semaphore()

    @pl.loop(1, devices)
    def _(step):
        pl.semaphore_signal(
            barrier, inc=1, device_id=(chain, lax.rem(tile + step, devices)), device_id_type=MESH
        )

    sibling = tile + 1 - 2 * lax.rem(tile, 2)
    turns = devices // 2

    def copy_to(peer, source, target, send_sem, recv_sem):
        return pltpu.make_async_remote_copy(
            src_ref=source,
            dst_ref=target,
            send_sem=send_sem,
            recv_sem=recv_sem,
            device_id=(chain, peer),
            device_id_type=MESH,
        )

    def ahead(first, turn):
        return lax.rem(first + 2 * turn, devices)

    def behind(first, turn):
        return lax.rem(first + devices - 2 * turn, devices)

    def outward(turn):
        peer = ahead(tile, turn)
        slot = 2 * turn
        source = grad_ref.at[plane_and_part(peer, planes)[0]]
        return copy_to(peer, source, arrived.at[slot], send_one.at[slot], recv_one.at[slot])

    def forward(turn):
        slot = 2 * turn + 1
        return copy_to(
            sibling, arrived.at[2 * turn], arrived.at[slot], send_one.at[slot], recv_one.at[slot]
        )

    def homeward(turn):
        slot = 2 * turn
        return copy_to(
            ahead(tile, turn), leaving.at[slot], partial.at[slot], send_two.at[slot], recv_two.at[slot]
        )

    def across(turn):
        slot = 2 * turn + 1
        return copy_to(
            sibling, leaving.at[slot], partial.at[slot], send_two.at[slot], recv_two.at[slot]
        )

    spectrum[...] = jnp.zeros(spectrum.shape, jnp.float32)
    pl.semaphore_wait(barrier, devices - 1)

    @pl.loop(1, turns)
    def _(turn):
        outward(turn).start()

    arrived[0] = grad_ref[plane]
    forward(0).start()
    load.wait()
    y_high[...], y_low[...] = halves(y_table[...])

    def block_rows(owner):
        return pl.ds(pl.multiple_of(owner // GY * x_rows, x_rows), x_rows)

    def table_rows(owner):
        return pl.ds(pl.multiple_of(lax.rem(owner, GY) * y_cols, y_cols), y_cols)

    def transform(owner, value):
        lines = table_rows(owner)
        spectrum[block_rows(owner), :] += dot_halves(
            halves(value), (y_high[lines, :], y_low[lines, :])
        )

    transform(tile, grad_ref[plane])

    def take_forwarded(turn):
        forward(turn).wait_recv()
        transform(behind(sibling, turn), arrived[2 * turn + 1])

    @pl.loop(1, turns)
    def _(turn):
        outward(turn).wait_recv()
        forward(turn).start()
        transform(behind(tile, turn), arrived[2 * turn])
        take_forwarded(turn - 1)

    take_forwarded(turns - 1)

    def along_x(value, orient):
        mixed = dot_halves((x_high_ref[...], x_low_ref[...]), halves(value))
        cosine, sine = mixed[0:x_total], mixed[x_total:]
        real = cosine[:, 0:width] - orient * sine[:, width:]
        imag = cosine[:, width:] + orient * sine[:, 0:width]
        return real, imag

    real, imag = along_x(spectrum[...], -1.0)
    spectrum[:, 0:width] = real * mass_ref[...]
    spectrum[:, width:] = imag * mass_ref[...]
    real, imag = along_x(spectrum[...], 1.0)
    back_high[:, 0:width], back_low[:, 0:width] = halves(real)
    back_high[:, width:], back_low[:, width:] = halves(imag)

    def restored(owner):
        rows, lines = block_rows(owner), table_rows(owner)
        return dot_halves(
            (back_high[rows, :], back_low[rows, :]), (y_high[lines, :], y_low[lines, :]), 1
        )

    def pass_across(turn):
        leaving[2 * turn + 1] = restored(ahead(sibling, turn))
        across(turn).start()

    pass_across(1)

    @pl.loop(1, turns)
    def _(turn):
        pass_across(lax.rem(turn + 1, turns))
        own = restored(ahead(tile, turn))
        across(turn).wait_recv()
        leaving[2 * turn] = own + partial[2 * turn + 1]
        homeward(turn).start()

    out_ref[...] = jnp.zeros(out_ref.shape, jnp.float32)
    mine = restored(tile)
    across(0).wait_recv()
    out_ref[plane] += mine + partial[1]

    @pl.loop(1, turns)
    def _(turn):
        homeward(turn).wait_recv()
        out_ref[plane_and_part(behind(tile, turn), planes)[0]] += partial[2 * turn]

    forward(0).wait_send()
    across(0).wait_send()

    @pl.loop(1, turns)
    def _(turn):
        outward(turn).wait_send()
        forward(turn).wait_send()
        across(turn).wait_send()
        homeward(turn).wait_send()


def table_halves(table):
    high = table.astype(jnp.bfloat16)
    low = (table - high.astype(np.float64)).astype(jnp.bfloat16)
    return jnp.asarray(high), jnp.asarray(low)


def run_spectral(grad, mass):
    planes, x_rows, y_cols = grad.shape
    devices = lax.axis_size("gx")
    x_total, width = mass.shape
    y_total = y_cols * GY
    parts = y_total // width
    turn = np.arange(x_total)[:, None] * np.arange(x_total)[None, :] % x_total
    angle = turn * (2.0 * np.pi / x_total)
    x_tables = table_halves(np.concatenate((np.cos(angle), np.sin(angle)), axis=0))
    turn = np.arange(y_total)[:, None] * np.arange(y_total)[None, :] % y_total
    angle = (turn * (2.0 * np.pi / y_total)).reshape(y_total, parts, width).transpose(1, 0, 2)
    y_table = np.concatenate((np.cos(angle), -np.sin(angle)), axis=2).astype(np.float32)
    vmem = pl.BlockSpec(memory_space=pltpu.VMEM)
    hbm = pl.BlockSpec(memory_space=pl.ANY)
    tiles = (devices, x_rows, y_cols)
    return pl.pallas_call(
        spectral_kernel,
        out_shape=jax.ShapeDtypeStruct(grad.shape, jnp.float32),
        in_specs=[vmem] * 4 + [hbm],
        out_specs=vmem,
        scratch_shapes=[
            pltpu.VMEM(tiles, jnp.float32),
            pltpu.VMEM((x_total, 2 * width), jnp.float32),
            pltpu.VMEM((y_total, 2 * width), jnp.float32),
            pltpu.VMEM((y_total, 2 * width), jnp.bfloat16),
            pltpu.VMEM((y_total, 2 * width), jnp.bfloat16),
            pltpu.VMEM((x_total, 2 * width), jnp.bfloat16),
            pltpu.VMEM((x_total, 2 * width), jnp.bfloat16),
            pltpu.VMEM(tiles, jnp.float32),
            pltpu.VMEM(tiles, jnp.float32),
            pltpu.SemaphoreType.DMA((devices,)),
            pltpu.SemaphoreType.DMA((devices,)),
            pltpu.SemaphoreType.DMA((devices,)),
            pltpu.SemaphoreType.DMA((devices,)),
            pltpu.SemaphoreType.DMA,
        ],
        compiler_params=pltpu.CompilerParams(
            collective_id=1, has_side_effects=True, vmem_limit_bytes=57 * 2**20
        ),
    )(grad, mass, *x_tables, jnp.asarray(y_table))


def pick_factor(length):
    candidate = math.isqrt(length)
    if candidate * candidate < length:
        candidate = candidate + 1
    while length % candidate != 0:
        candidate = candidate + 1
    return candidate


def phase_tables(rows_count, cols_count, modulus):
    first = jnp.arange(rows_count, dtype=jnp.int32)
    second = jnp.arange(cols_count, dtype=jnp.int32)
    phase_int = first[:, None] * second[None, :] % modulus
    angle_rad = phase_int.astype(jnp.float32) * (2.0 * math.pi / modulus)
    return (jnp.cos(angle_rad), jnp.sin(angle_rad))


def complex_mix(form, tab_cos, tab_sin, real_part, imag_part, orient):

    def product(table, data):
        return jnp.einsum(
            form, table, data, precision=lax.Precision.HIGHEST, preferred_element_type=jnp.float32
        )

    out_real = product(tab_cos, real_part) - orient * product(tab_sin, imag_part)
    out_imag = product(tab_cos, imag_part) + orient * product(tab_sin, real_part)
    return (out_real, out_imag)


def transform_rows(real_part, imag_part, orient):
    length, width = real_part.shape
    outer_len = pick_factor(length)
    inner_len = length // outer_len
    data_re = real_part.reshape(outer_len, inner_len, width)
    data_im = imag_part.reshape(outer_len, inner_len, width)
    cos_outer, sin_outer = phase_tables(outer_len, outer_len, outer_len)
    mid_re, mid_im = complex_mix("ca,abm->cbm", cos_outer, sin_outer, data_re, data_im, orient)
    twist_cos, twist_sin = phase_tables(outer_len, inner_len, length)
    twist_cos = twist_cos[:, :, None]
    twist_sin = twist_sin[:, :, None]
    turned_re = mid_re * twist_cos - orient * mid_im * twist_sin
    turned_im = mid_im * twist_cos + orient * mid_re * twist_sin
    cos_inner, sin_inner = phase_tables(inner_len, inner_len, inner_len)
    final_re, final_im = complex_mix(
        "db,cbm->dcm", cos_inner, sin_inner, turned_re, turned_im, orient
    )
    return (final_re.reshape(length, width), final_im.reshape(length, width))


def per_device(
    courant, ckpt_prev, ckpt_cur, adj_next, adj_cur, rec_x, rec_plane, traces, mass_kernel
):
    x_rows, z_depth, y_cols = courant.shape[1:]
    devices = lax.axis_size("gx")
    x_blocks = devices // GY
    x_total = x_rows * x_blocks
    y_total = y_cols * GY
    cell_y = rec_plane % y_total
    cell_z = rec_plane // y_total
    owner = rec_x // x_rows * GY + cell_y // y_cols
    cell_row = (owner * x_rows + rec_x % x_rows) * z_depth + cell_z
    records = jnp.concatenate(
        (
            cell_row.astype(jnp.float32)[None],
            (cell_y % y_cols).astype(jnp.float32)[None],
            traces,
            jnp.zeros((6 - STEPS, rec_x.shape[0]), jnp.float32),
        ),
        axis=0,
    )
    dense = x_total <= 512 and GY == 2 * z_depth and devices % z_depth == 0
    mass = mass_kernel.reshape(-1, 128) if dense else jnp.zeros((8, 128), jnp.float32)
    gradient, adj_now, adj_later, mass_slots = run_window(
        *(
            field.reshape(x_rows * z_depth, y_cols)
            for field in (courant, ckpt_prev, ckpt_cur, adj_next, adj_cur)
        ),
        records,
        mass,
        dense,
    )
    tile_shape = (1, x_rows, z_depth, y_cols)
    if dense:
        by_plane = gradient.reshape(x_rows, z_depth, y_cols).transpose(1, 0, 2)
        part_mass = mass_slots.reshape(z_depth, x_total, -1).transpose(1, 0, 2)
        part_mass = part_mass.reshape(x_total, -1) * (1.0 / (x_total * y_total))
        scaled = run_spectral(by_plane, part_mass).transpose(1, 0, 2)
        return (
            scaled.reshape(tile_shape),
            adj_now.reshape(tile_shape),
            adj_later.reshape(tile_shape),
        )
    flat_grad = gradient.reshape(x_rows * z_depth, 1, y_cols)
    rows = lax.all_to_all(flat_grad, "gx", split_axis=0, concat_axis=1, tiled=True)
    share = rows.shape[0]
    lines = rows.reshape(share * x_blocks, y_total).T
    spec_re_t, spec_im_t = transform_rows(lines, jnp.zeros_like(lines), -1.0)
    spec_re = spec_re_t.T.reshape(share, x_blocks, y_total)
    spec_im = spec_im_t.T.reshape(share, x_blocks, y_total)
    cols_re, cols_im = (
        lax.all_to_all(spec_re, "gx", split_axis=2, concat_axis=0, tiled=True),
        lax.all_to_all(spec_im, "gx", split_axis=2, concat_axis=0, tiled=True),
    )
    col_width = cols_re.shape[2]
    half_width = z_depth * col_width

    def to_columns(part):
        return (
            part.reshape(x_rows, z_depth, x_blocks, col_width)
            .transpose(2, 0, 1, 3)
            .reshape(x_total, half_width)
        )

    def from_columns(part):
        return (
            part.reshape(x_blocks, x_rows, z_depth, col_width)
            .transpose(1, 2, 0, 3)
            .reshape(devices * share, x_blocks, col_width)
        )

    freq_re, freq_im = transform_rows(to_columns(cols_re), to_columns(cols_im), -1.0)
    kernel_scale = (
        jnp.broadcast_to(mass_kernel[:, None, :], (x_total, z_depth, col_width)).reshape(
            x_total, half_width
        )
        / x_total
    )
    freq_re = freq_re * kernel_scale
    freq_im = freq_im * kernel_scale
    spat_re, spat_im = transform_rows(freq_re, freq_im, 1.0)
    back_re = from_columns(spat_re)
    back_im = from_columns(spat_im)
    line_re, line_im = (
        lax.all_to_all(back_re, "gx", split_axis=0, concat_axis=2, tiled=True),
        lax.all_to_all(back_im, "gx", split_axis=0, concat_axis=2, tiled=True),
    )
    lines_re = line_re.reshape(share * x_blocks, y_total).T
    lines_im = line_im.reshape(share * x_blocks, y_total).T
    real_t, imag_t = transform_rows(lines_re, lines_im, 1.0)
    real_lines = (real_t.T / y_total).reshape(share, devices, y_cols)
    tiled = lax.all_to_all(real_lines, "gx", split_axis=1, concat_axis=0, tiled=True)
    return (tiled.reshape(tile_shape), adj_now.reshape(tile_shape), adj_later.reshape(tile_shape))


def solution(mesh):
    in_specs = (
        P(("chain", "gx"), None, None, None),
        P(("chain", "gx"), None, None, None),
        P(("chain", "gx"), None, None, None),
        P(("chain", "gx"), None, None, None),
        P(("chain", "gx"), None, None, None),
        P(("chain", "gx")),
        P(("chain", "gx")),
        P(None, ("chain", "gx")),
        P(None, "gx"),
    )
    out_specs = (
        P(("chain", "gx"), None, None, None),
        P(("chain", "gx"), None, None, None),
        P(("chain", "gx"), None, None, None),
    )
    return jax.shard_map(
        per_device, mesh=mesh, in_specs=in_specs, out_specs=out_specs, check_vma=False
    )
```
